256 devices in a mesh: mp: 16 (over x, z_hi, core), scen: 16 (over z_lo, y).
Axes of the slice: x: 4, y: 4, z: 8 (z_hi: 2, z_lo: 4; z = z_hi * 4 + z_lo), core: 2. Of those that a mesh axis runs over, the one named last changes fastest.
Arguments:
- group_id: int32 [16384], P('mp'), may hold values from 0 to 255
- issue_state: int32 [16384], P('mp'), may hold values from 0 to 7
- account_start: float32 [16384], P('mp'), may hold values from 0.3 to 3
- transition: float32 [256, 8, 8], replicated, may hold values from 0 to 1
- lapse_base: float32 [256], replicated, may hold values from 0.005 to 0.05
- benefit: float32 [8], replicated, may hold values from 0.002 to 0.05
- bond_block: int32 [40960, 1], P('mp'), may hold values from 0 to 255
- bond_flows: float32 [40960, 256], P('mp'), may hold values from 0 to 0.02
- bond_target: float32 [40960], P('mp'), may hold values from 0.7 to 1.4
- base_rate: float32 [2048], P('scen'), may hold values from 0.01 to 0.06
- rate_moves: float32 [3, 2048], P(None, 'scen'), may hold values from -0.012 to 0.012
- guarantee: float32 [256], replicated, may hold values from 0 to 0.035
- spread: float32 [256], replicated, may hold values from 0 to 0.03
- start_rate: float32 [2048, 256], P('scen'), may hold values from 0 to 0.05
Outputs:
- occupancy: float32 [8, 2048, 16384], P(None, 'scen', 'mp')
- account_value: float32 [2048, 16384], P('scen', 'mp')
- credited_pct: float32 [2048, 256], P('scen', 'mp')
- outflow_value: float32 [256], P('mp')
The draws below stay inside these ranges and needn't reach their ends.
All inputs are finite; a program needn't handle non-finite values.
Results may differ from the reference program's by a relative error of at most 0.0003.
Values sent between devices are 32-bit elements; how exact they have to be, the bound alone decides.
A program may use at most 128 MiB of HBM per device.

```python
import math
import jax
import jax.numpy as jnp
from jax import lax

S = 8
PG = 256
K = 256
MONTHS = 3
MPTS = 16384
SCEN = 2048
BONDS = 40960


def plant(values, key, smallest, largest):
    longest = values.shape.index(max(values.shape))
    spots = []
    for shift in (0, 1):
        where = [jax.random.randint(jax.random.fold_in(key, axis), (), 0, length) for axis, length in enumerate(values.shape)]
        where[longest] = (where[longest] + shift) % values.shape[longest]
        spots.append(tuple(where))
    return values.at[spots[0]].set(smallest).at[spots[1]].set(largest)


def levels(stream_key, dims, split, least, top_value):
    gain, own = 1.0, jax.random.fold_in(stream_key, 6)
    for dim, shards_of in split:
        heights = jnp.exp(jax.random.uniform(jax.random.fold_in(own, dim), (shards_of,), jnp.float32, least / len(split), top_value / len(split)))
        gain = gain * jnp.repeat(heights, dims[dim] // shards_of).reshape([-1 if axis == dim else 1 for axis in range(len(dims))])
    return gain


def different_ones(own_key, rows, count, top, lift):
    order = jax.random.permutation(jax.random.fold_in(own_key, 1), count)
    favour = order
    for power in range(3):
        favour = favour * favour // count
    favour = favour * lift // count
    chance = jax.random.randint(jax.random.fold_in(own_key, 2), (rows, count), 0, 4096) + favour
    holders = jax.random.permutation(jax.random.fold_in(own_key, 3), rows)[jnp.arange(count) % rows]
    chance = jnp.where(jnp.arange(rows)[:, None] == holders[None, :], 1 << 14, chance)
    score = chance * count + jnp.arange(count)
    return lax.top_k(score.astype(jnp.int32), top)[1].astype(jnp.int32)


def normal_values(own_key, shape, width, limit, split=(), kind=jnp.bfloat16):
    loudness = levels(own_key, shape, split, -0.22, 0.18) if split else 1.0
    values = jax.random.normal(own_key, shape, jnp.float32) * width * loudness
    return jnp.minimum(jnp.maximum(values, -limit), limit).astype(kind)


def setup_inputs(seed: int = 0) -> dict:
    keys = jax.random.split(jax.random.key(seed), 15)
    group_id = plant(jax.random.randint(keys[0], (MPTS,), 0, PG), jax.random.fold_in(keys[0], 1), 0, PG - 1).astype(jnp.int32)
    issue_state = plant(jax.random.randint(keys[1], (MPTS,), 0, S), jax.random.fold_in(keys[1], 1), 0, S - 1).astype(jnp.int32)
    account_start = jnp.clip(jnp.exp(math.log(3.0) - 2.3025851 * jax.random.uniform(keys[2], (MPTS,), jnp.float32) ** levels(keys[2], (MPTS,), ((0, 16),), -0.2, 0.2)), 0.3, 3.0)
    transition = jnp.clip(jax.random.uniform(keys[3], (PG, S, S), jnp.float32, 0.0, 1.0), 0.0, 1.0)
    lapse_base = jnp.clip(jnp.exp(jax.random.uniform(keys[4], (PG,), jnp.float32, math.log(0.005), math.log(0.05))), 0.005, 0.05)
    benefit = jnp.clip(jnp.exp(jax.random.uniform(keys[5], (S,), jnp.float32, math.log(0.002), math.log(0.05))), 0.002, 0.05)
    bond_block = different_ones(keys[6], BONDS, PG, 1, 0)
    bond_flows = jnp.clip(0.02 * jax.random.uniform(keys[7], (BONDS, K), jnp.float32) ** levels(keys[7], (BONDS, K), ((0, 16),), -0.2, 0.2), 0.0, 0.02)
    bond_target = jnp.clip(jnp.exp(math.log(1.4) - 0.6931472 * jax.random.uniform(keys[8], (BONDS,), jnp.float32) ** levels(keys[8], (BONDS,), ((0, 16),), -0.2, 0.2)), 0.7, 1.4)
    base_rate = jnp.clip(0.01 + 0.04999999888241291 * jax.random.uniform(keys[9], (SCEN,), jnp.float32) ** levels(keys[9], (SCEN,), ((0, 16),), -0.2, 0.2), 0.01, 0.06)
    rate_moves = normal_values(keys[10], (MONTHS, SCEN), 0.002, 0.012, ((1, 16),), jnp.float32)
    guarantee = jnp.clip(jax.random.uniform(keys[11], (PG,), jnp.float32, 0.0, 0.035), 0.0, 0.035)
    spread = jnp.clip(jax.random.uniform(keys[12], (PG,), jnp.float32, 0.0, 0.03), 0.0, 0.03)
    start_rate = jnp.clip(0.05 * jax.random.uniform(keys[13], (SCEN, PG), jnp.float32) ** levels(keys[13], (SCEN, PG), ((0, 16),), -0.2, 0.2), 0.0, 0.05)
    return {"group_id": group_id, "issue_state": issue_state, "account_start": account_start, "transition": transition, "lapse_base": lapse_base, "benefit": benefit, "bond_block": bond_block, "bond_flows": bond_flows, "bond_target": bond_target, "base_rate": base_rate, "rate_moves": rate_moves, "guarantee": guarantee, "spread": spread, "start_rate": start_rate}


EXACT = lax.Precision.HIGHEST
STAY_WEIGHT = 40.0
LAPSE_SLOPE = 30.0
LIQUID_CHARGE = 0.5


def discount(rate_now, date_index):
    horizon = jnp.arange(K, dtype=jnp.int32)
    tenor = (horizon - date_index + 1).astype(jnp.float32) / 12.0
    live = horizon >= date_index
    factor = jnp.exp(-rate_now[:, None] * tenor[None, :])
    return jnp.where(live[None, :], factor, jnp.zeros_like(factor))


def asset_values(rate_now, date_index, bond_flows, bond_target, bond_member):
    raw_prices = jnp.dot(discount(rate_now, date_index), bond_flows.T, precision=EXACT)
    mean_price = jnp.sum(raw_prices, axis=0) / SCEN
    scaled = raw_prices * (bond_target / mean_price)[None, :]
    return jnp.dot(scaled, bond_member, precision=EXACT)


def reference(group_id, issue_state, account_start, transition, lapse_base, benefit, bond_block, bond_flows, bond_target, base_rate, rate_moves, guarantee, spread, start_rate):
    labels = jnp.arange(PG, dtype=jnp.int32)
    member = (group_id[:, None] == labels[None, :]).astype(jnp.float32)
    bond_member = (bond_block[:, 0][:, None] == labels[None, :]).astype(jnp.float32)
    stochastic = transition + STAY_WEIGHT * jnp.eye(S, dtype=jnp.float32)[None]
    stochastic = stochastic / jnp.sum(stochastic, axis=2, keepdims=True)
    point_moves = jnp.dot(member, stochastic.reshape(PG, S * S), precision=EXACT).T.reshape(S, S, -1)
    point_lapse = jnp.dot(member, lapse_base, precision=EXACT)
    rate_path = [base_rate]
    for step_month in range(MONTHS):
        rate_path.append(rate_path[-1] + rate_moves[step_month])
    states = jnp.arange(S, dtype=jnp.int32)
    start_mass = (issue_state[None, :] == states[:, None]).astype(jnp.float32)
    occupancy = jnp.broadcast_to(start_mass[:, None, :], (S, SCEN, MPTS))
    account_value = jnp.broadcast_to(account_start[None, :], (SCEN, MPTS))
    credited = start_rate
    present = jnp.zeros((SCEN, PG), jnp.float32)
    for step_month in range(MONTHS):
        point_rate = jnp.dot(credited, member.T, precision=EXACT)
        lapse_rate = point_lapse[None, :] * 2.0 * jax.nn.sigmoid(LAPSE_SLOPE * (rate_path[step_month][:, None] - point_rate))
        lapsed_mass = occupancy[0] * lapse_rate
        kept_mass = jnp.concatenate([(occupancy[0] - lapsed_mass)[None], occupancy[1:]], axis=0)
        occupancy = jnp.einsum('scm,sum->ucm', kept_mass, point_moves, precision=EXACT)
        account_value = account_value * (1.0 + point_rate / 12.0)
        paid_share = jnp.einsum('u,ucm->cm', benefit, occupancy, precision=EXACT)
        outflow = account_value * (lapsed_mass + paid_share)
        group_flows = jnp.dot(outflow, member, precision=EXACT)
        held_value = asset_values(rate_path[step_month], step_month, bond_flows, bond_target, bond_member)
        income = jnp.dot(bond_flows[:, step_month], bond_member, precision=EXACT)
        later_value = asset_values(rate_path[step_month + 1], step_month + 1, bond_flows, bond_target, bond_member) + income[None, :]
        earned = 12.0 * (later_value - held_value) / held_value
        credited = jnp.maximum(guarantee[None, :], 0.5 * credited + 0.5 * (earned - spread[None, :]) - LIQUID_CHARGE * group_flows / held_value)
        present = present + group_flows * jnp.exp(-rate_path[step_month + 1] * (step_month + 1) / 12.0)[:, None]
    return occupancy, account_value, 100.0 * credited, jnp.sum(present, axis=0) / SCEN
```

```python
import jax
import jax.numpy as jnp
from jax import lax
from jax.sharding import PartitionSpec as P

EXACT = lax.Precision.HIGHEST
STAY_WEIGHT = 40.0
LAPSE_SLOPE = 30.0
LIQUID_CHARGE = 0.5


def dot(a, b):
    return jnp.dot(a, b, precision=EXACT)


def body(
    group_id,
    issue_state,
    account_start,
    transition,
    lapse_base,
    benefit,
    bond_block,
    bond_flows,
    bond_target,
    base_rate,
    rate_moves,
    guarantee,
    spread,
    start_rate,
):
    group_count, state_count = transition.shape[:2]
    scen_dev = base_rate.shape[0]
    scen_axis, mp_axis = lax.axis_size("scen"), lax.axis_size("mp")
    scen_all = scen_dev * scen_axis
    month_count = rate_moves.shape[0]
    term_count = bond_flows.shape[1]
    owned = group_count // mp_axis
    first_group = lax.axis_index("mp") * owned
    term_dev = term_count // scen_axis
    labels = jnp.arange(group_count, dtype=jnp.int32)

    def own_rows(array):
        return lax.dynamic_slice_in_dim(array, first_group, owned, 0)

    rate_path = [base_rate]
    for month in range(month_count):
        rate_path.append(rate_path[-1] + rate_moves[month])
    horizon = jnp.arange(term_count, dtype=jnp.int32)
    discounts = []
    for date in range(month_count + 1):
        tenor = (horizon - date + 1).astype(jnp.float32) / 12.0
        factor = jnp.exp(-tenor[:, None] * rate_path[date][None, :])
        discounts.append(jnp.where((horizon >= date)[:, None], factor, 0.0))
    discounts = jnp.stack(discounts)
    mean_discount = lax.psum(jnp.sum(discounts, axis=2), "scen") / scen_all

    mean_price = dot(mean_discount, bond_flows.T)
    weight = bond_target[None, :] / mean_price
    bond_member = (bond_block[:, 0][None, :] == labels[:, None]).astype(jnp.float32)
    first_term = lax.axis_index("scen") * term_dev
    flows_dev = lax.dynamic_slice_in_dim(bond_flows.T, first_term, term_dev, 0)
    scaled = (weight[:, None, :] * flows_dev[None, :, :]).reshape(-1, flows_dev.shape[1])
    worth = dot(bond_member, scaled.T)
    income = dot(bond_member, bond_flows[:, :month_count])

    member = (group_id[None, :] == labels[:, None]).astype(jnp.float32)
    states = jnp.arange(state_count, dtype=jnp.int32)
    start_mass = (issue_state[None, :] == states[:, None]).astype(jnp.float32)
    accounts = dot(member, (start_mass * account_start[None, :]).T)
    summed = lax.psum_scatter(
        jnp.concatenate([worth, income, accounts], axis=1), "mp", scatter_dimension=0, tiled=True
    )
    width = worth.shape[1]
    income, accounts = summed[:, width : width + month_count], summed[:, width + month_count :]
    worth = lax.all_gather(summed[:, :width].reshape(owned, month_count + 1, term_dev), "scen", axis=2, tiled=True)
    assets = [dot(worth[:, date], discounts[date]) for date in range(month_count + 1)]

    move = transition + STAY_WEIGHT * jnp.eye(state_count, dtype=jnp.float32)[None]
    move = move / jnp.sum(move, axis=2, keepdims=True)
    powers = [move]
    for _ in range(month_count - 1):
        powers.append(jnp.sum(powers[-1][:, :, :, None] * move[:, None, :, :], axis=2))

    own_powers = [own_rows(power) for power in powers]
    own_starts = [accounts[:, 0]] + [jnp.sum(accounts * power[:, :, 0], axis=1) for power in own_powers]
    own_pays = [jnp.sum(power * benefit[None, None, :], axis=2) for power in own_powers]
    own_start_pays = [jnp.sum(accounts * pay, axis=1) for pay in own_pays]

    credited = own_rows(start_rate.T)
    path = [credited]
    lapse_own, guarantee_own, spread_own = own_rows(lapse_base), own_rows(guarantee), own_rows(spread)
    growth = jnp.ones_like(credited)
    lapses = []
    present = jnp.zeros_like(credited)
    for month in range(month_count):
        factor = lapse_own[:, None] * 2.0 * jax.nn.sigmoid(LAPSE_SLOPE * (rate_path[month][None, :] - credited))
        first = own_starts[month][:, None]
        for lag, lapse in enumerate(reversed(lapses)):
            first = first - lapse * own_powers[lag][:, 0, 0][:, None]
        lapses.append(first * factor)
        growth = growth * (1.0 + credited / 12.0)
        paid = own_start_pays[month][:, None]
        for lag, lapse in enumerate(reversed(lapses)):
            paid = paid - lapse * own_pays[lag][:, 0][:, None]
        flows = growth * (lapses[-1] + paid)
        held = assets[month]
        later = assets[month + 1] + income[:, month][:, None]
        earned = 12.0 * (later - held) / held
        credited = jnp.maximum(
            guarantee_own[:, None],
            0.5 * credited + 0.5 * (earned - spread_own[:, None]) - LIQUID_CHARGE * flows / held,
        )
        path.append(credited)
        present = present + flows * jnp.exp(-rate_path[month + 1] * (month + 1) / 12.0)[None, :]
    outflow_value = lax.psum(jnp.sum(present, axis=1), "scen") / scen_all

    others = lax.all_gather(jnp.stack(path[1:month_count]), "mp", axis=1, tiled=True)
    rates = [start_rate] + [others[month].T for month in range(month_count - 1)]
    growth = jnp.ones_like(start_rate)
    tables = []
    for month in range(month_count):
        tables.append(
            lapse_base[None, :]
            * 2.0
            * jax.nn.sigmoid(LAPSE_SLOPE * (rate_path[month][:, None] - rates[month]))
        )
        growth = growth * (1.0 + rates[month] / 12.0)
    points = dot(jnp.concatenate(tables + [growth]), member).reshape(month_count + 1, scen_dev, -1)
    point_powers = [
        dot(power.transpose(1, 2, 0).reshape(-1, group_count), member).reshape(state_count, state_count, -1)
        for power in powers
    ]
    own_state = [jnp.sum(start_mass[:, None, :] * power, axis=0) for power in point_powers]
    lapses = []
    for month in range(month_count):
        first = (start_mass[0] if month == 0 else own_state[month - 1][0])[None, :]
        for lag, lapse in enumerate(reversed(lapses)):
            first = first - lapse * point_powers[lag][0, 0][None, :]
        lapses.append(first * points[month])
    occupancy = own_state[-1][:, None, :]
    for lag, lapse in enumerate(reversed(lapses)):
        occupancy = occupancy - lapse[None] * point_powers[lag][0][:, None, :]
    account_value = account_start[None, :] * points[month_count]
    return (occupancy, account_value, 100.0 * credited.T, outflow_value)


def solution(mesh):
    placed = (
        P("mp"),
        P("mp"),
        P("mp"),
        P(),
        P(),
        P(),
        P("mp", None),
        P("mp", None),
        P("mp"),
        P("scen"),
        P(None, "scen"),
        P(),
        P(),
        P("scen", None),
    )
    return jax.shard_map(
        body,
        mesh=mesh,
        in_specs=placed,
        out_specs=(P(None, "scen", "mp"), P("scen", "mp"), P("scen", "mp"), P("mp")),
        check_vma=False,
    )
```

```python
import functools

import jax
import jax.numpy as jnp
from jax import lax
from jax.experimental import pallas as pl
from jax.experimental.pallas import tpu as pltpu
from jax.sharding import PartitionSpec as P

MESH = pl.DeviceIdType.MESH
EXACT = lax.Precision.HIGHEST
F32, BF16 = jnp.float32, jnp.bfloat16
STAY_WEIGHT = 40.0
LAPSE_SLOPE = 30.0
LIQUID_CHARGE = 0.5

S = 8
PG = 256
K = 256
DATES = 4
MONTHS = 3
C = 128
M = 1024
B = 2560
TILE = 256
MP = 16
SC = 16
SCEN = C * SC
KD = K // SC
GQ = 2 * PG // MP
VMEM_LIMIT = 48 * 1024 * 1024

NT = (((1,), (1,)), ((), ()))
NN = (((1,), (0,)), ((), ()))


def dot(a, b, dims, precision=None):
    return lax.dot_general(a, b, dims, precision=precision, preferred_element_type=F32)


def parts(x, count):
    found = []
    for _ in range(count):
        found.append(x.astype(BF16))
        x = x - found[-1].astype(F32)
    return found


def stack_parts(x, count, rows):
    found = parts(x, count)
    pieces = [piece.astype(F32) for piece in found]
    rest = rows - count * x.shape[0]
    if rest:
        pieces.append(jnp.zeros((rest, x.shape[1]), F32))
    return jnp.concatenate(pieces, axis=0).astype(BF16)


def iota(shape, axis):
    return lax.broadcasted_iota(jnp.int32, shape, axis)


def group_at(place):
    block = place // 16
    return (block // 4 * 4 + block % 2 * 2 + block // 2 % 2) * 16 + place % 16


def swap_blocks(rows):
    block = iota(rows.shape, 1) // 16 % 4
    width = rows.shape[1]
    up = pltpu.roll(rows, width - 16, 1)
    down = pltpu.roll(rows, 16, 1)
    return jnp.where(block == 1, up, jnp.where(block == 2, down, rows))


def discounts(rates, date):
    horizon = iota((K, C), 0)
    tenor = (horizon - date + 1).astype(F32) / 12.0
    factor = jnp.exp(-tenor * rates[date : date + 1, :])
    return jnp.where(horizon >= date, factor, 0.0) if date else factor


def exchange_kernel(
    group_ref,
    state_ref,
    account_ref,
    transition_ref,
    rows_ref,
    benefit_ref,
    block_ref,
    flows_hbm,
    target_ref,
    base_ref,
    moves_ref,
    start_ref,
    rho_ref,
    pre_ref,
    table_ref,
    credited_ref,
    value_ref,
    path_ref,
    flows_ref,
    flow_parts,
    chosen_ref,
    bond_ref,
    point_ref,
    disc_ref,
    cols_ref,
    first_ref,
    a_src,
    a_buf,
    e_src,
    e_buf,
    b_src,
    b_buf,
    c_buf,
    d_buf,
    f_src,
    f_buf,
    load_sem,
    a_send,
    a_recv,
    e_send,
    e_recv,
    b_send,
    b_recv,
    c_send,
    c_recv,
    d_send,
    d_recv,
    f_send,
    f_recv,
):
    mp, sc = lax.axis_index("mp"), lax.axis_index("scen")
    x, zh, core = mp // 4, mp // 2 % 2, mp % 2
    own = x * 2 + core
    zl, y = sc // 4, sc % 4

    def mp_index(dx, dz, dc):
        return (x + dx) % 4 * 4 + (zh + dz) % 2 * 2 + (core + dc) % 2

    mp_peers = [
        mp_index(dx, dz, dc) for dz in (1, 0) for dx in (2, 1, 3, 0) for dc in (0, 1) if (dx, dz, dc) != (0, 0, 0)
    ]
    near_peers = [mp_index(dx, 0, dc) for dx in (2, 1, 3, 0) for dc in (0, 1) if (dx, dc) != (0, 0)]
    sc_peers = [
        (zl + dz) % 4 * 4 + (y + dy) % 4 for dz in (2, 1, 3, 0) for dy in (2, 1, 3, 0) if (dz, dy) != (0, 0)
    ]

    barrier = pltpu.get_barrier_semaphore()
    for peer in mp_peers:
        pl.semaphore_signal(barrier, inc=1, device_id=(peer, sc), device_id_type=MESH)
    for peer in sc_peers:
        pl.semaphore_signal(barrier, inc=1, device_id=(mp, peer), device_id_type=MESH)
    load = pltpu.make_async_copy(flows_hbm, flows_ref, load_sem)
    load.start()

    def to_scen(src, dst, send, recv):
        return [
            pltpu.make_async_remote_copy(
                src_ref=src, dst_ref=dst, send_sem=send.at[n], recv_sem=recv.at[sc],
                device_id=(mp, peer), device_id_type=MESH,
            )
            for n, peer in enumerate(sc_peers)
        ]

    def from_scen(src, slot, send, recv):
        for n, peer in enumerate(sc_peers):
            pltpu.make_async_remote_copy(
                src_ref=src, dst_ref=slot(peer), send_sem=send.at[n], recv_sem=recv.at[peer],
                device_id=(mp, peer), device_id_type=MESH,
            ).wait_recv()

    def to_mp(src, dst, send, recv, peers, mark):
        return [
            pltpu.make_async_remote_copy(
                src_ref=src(peer), dst_ref=dst, send_sem=send.at[n], recv_sem=recv.at[mark],
                device_id=(peer, sc), device_id_type=MESH,
            )
            for n, peer in enumerate(peers)
        ]

    def from_mp(src, slot, send, recv, peers, mark):
        for n, peer in enumerate(peers):
            pltpu.make_async_remote_copy(
                src_ref=src(peer), dst_ref=slot(peer), send_sem=send.at[n], recv_sem=recv.at[mark(peer)],
                device_id=(peer, sc), device_id_type=MESH,
            ).wait_recv()

    def pair(index):
        return index // 4 * 2 + index % 2

    rates = [base_ref[...]]
    for month in range(MONTHS):
        rates.append(rates[-1] + moves_ref[month : month + 1, :])
    rates = jnp.concatenate(rates, axis=0)
    path_ref[...] = jnp.concatenate([rates, jnp.zeros_like(rates)], axis=0)
    ones = jnp.ones((16, C), BF16)
    sums = []
    for date in range(DATES):
        pieces = parts(discounts(rates, date), 3)
        total = jnp.zeros((16, K), F32)
        for number, piece in enumerate(pieces):
            disc_ref[date, number] = piece
        for piece in reversed(pieces):
            total = total + dot(ones, piece, NT)
        sums.append(total[0:1])
    sums = jnp.concatenate(sums, axis=0)
    a_src[...] = jnp.concatenate([sums[:, : K // 2], sums[:, K // 2 :]], axis=0)

    pl.semaphore_wait(barrier, MP + SC - 2)
    sends = to_scen(a_src, a_buf.at[sc], a_send, a_recv)
    for copy in sends:
        copy.start()
    a_buf[sc] = a_src[...]

    load.wait()
    picks = iota((32, K), 0)
    wanted = jnp.where(picks < KD, sc * KD + picks, picks - KD)
    chosen = ((iota((32, K), 1) == wanted) & (picks < KD + MONTHS)).astype(BF16)
    bond_labels = group_at(iota((PG, TILE), 0))

    def prepare(tile, income):
        at = pl.ds(pl.multiple_of(tile * TILE, TILE), TILE)
        pieces = parts(flows_ref[at, :], 3)
        for number, piece in enumerate(pieces):
            flow_parts[number, at, :] = piece
        found = dot(chosen, pieces[2], NT) + dot(chosen, pieces[1], NT) + dot(chosen, pieces[0], NT)
        chosen_ref[:, at] = found[:KD]
        groups = (bond_labels == block_ref[:, at]).astype(BF16)
        bond_ref[:, at] = groups
        return income + dot(stack_parts(found[KD : KD + 8], 3, 32), groups, NT)

    income = lax.fori_loop(0, B // TILE, prepare, jnp.zeros((32, PG), F32))
    income = income[0:8] + income[8:16] + income[16:24]

    point_labels = iota((PG, TILE), 0)
    accounts = jnp.zeros((32, PG), F32)
    for tile in range(M // TILE):
        at = pl.ds(tile * TILE, TILE)
        groups = (point_labels == group_ref[:, at]).astype(BF16)
        point_ref[:, at] = groups
        mass = jnp.where(iota((S, TILE), 0) == state_ref[:, at], account_ref[:, at], 0.0)
        accounts = accounts + dot(stack_parts(mass, 3, 32), groups, NT)
    accounts = accounts[0:8] + accounts[8:16] + accounts[16:24]

    move = []
    for s in range(S):
        row = transition_ref[s] + jnp.where(iota((S, PG), 0) == s, STAY_WEIGHT, 0.0)
        move.append(row / jnp.sum(row, axis=0, keepdims=True))
    powers = [move]
    for _ in range(MONTHS - 1):
        last = powers[-1]
        powers.append([functools.reduce(jnp.add, [last[s][v : v + 1] * move[v] for v in range(S)]) for s in range(S)])
    benefit = jnp.zeros((S, PG), F32)
    for u in range(S):
        benefit = jnp.where(iota((S, PG), 0) == u, benefit_ref[u], benefit)
    stays = [jnp.concatenate([power[s][0:1] for s in range(S)], axis=0) for power in powers]
    pays = [
        jnp.concatenate([jnp.sum(power[s] * benefit, axis=0, keepdims=True) for s in range(S)], axis=0)
        for power in powers
    ]

    def by_state(rows):
        return jnp.sum(accounts * rows, axis=0, keepdims=True)

    early = [accounts[0:1], by_state(stays[0]), by_state(stays[1]), by_state(pays[0]), by_state(pays[1]), by_state(pays[2])]
    early = swap_blocks(jnp.concatenate(early + [jnp.zeros((2, PG), F32)], axis=0))
    for q in range(MP // 2):
        e_src[q] = jnp.concatenate(
            [early[:, q * GQ : (q + 1) * GQ], income[:, q * GQ : (q + 1) * GQ], jnp.zeros((8, C - 2 * GQ), F32)], axis=1
        )
    e_copies = to_mp(lambda peer: e_src.at[pair(peer)], e_buf.at[mp], e_send, e_recv, mp_peers, mp)
    for copy in e_copies:
        copy.start()
    sends += e_copies
    e_buf[mp] = e_src[own]

    from_scen(a_src, lambda peer: a_buf.at[peer], a_send, a_recv)
    mean = a_buf[0]
    for slot in range(1, SC):
        mean = mean + a_buf[slot]
    mean = mean * (1.0 / SCEN)
    mean = stack_parts(jnp.concatenate([mean[0:4], mean[4:8]], axis=1), 3, 16)

    def weigh(tile, total):
        at = pl.ds(pl.multiple_of(tile * TILE, TILE), TILE)
        high = dot(mean, flow_parts[0, at, :], NT)
        middle = dot(mean, flow_parts[1, at, :], NT)
        low = dot(mean, flow_parts[2, at, :], NT)
        price = high[0:4] + ((high[4:8] + middle[0:4]) + (high[8:12] + middle[4:8] + low[0:4]))
        weight = target_ref[:, at] / price
        flows = chosen_ref[:, at]
        scaled = jnp.concatenate([weight[date : date + 1] * flows for date in range(DATES)], axis=0)
        return total + dot(stack_parts(scaled, 3, 3 * DATES * KD), bond_ref[:, at], NT)

    worth = lax.fori_loop(0, B // TILE, weigh, jnp.zeros((3 * DATES * KD, PG), F32))
    size = DATES * KD
    worth = worth[0:size] + (worth[size : 2 * size] + worth[2 * size :])
    for q in range(MP // 2):
        b_src[q] = jnp.concatenate(
            [worth[date * KD : (date + 1) * KD, q * GQ : (q + 1) * GQ] for date in range(DATES)], axis=1
        )
    b_copies = to_mp(lambda peer: b_src.at[pair(peer)], b_buf.at[mp], b_send, b_recv, mp_peers, mp)
    for copy in b_copies:
        copy.start()
    sends += b_copies
    b_buf[mp] = b_src[own]

    local = [rows_ref[0:3], stays[0][0:1], stays[1][0:1], pays[0][0:1], pays[1][0:1], pays[2][0:1]]
    local = jnp.concatenate(local, axis=0)
    order = (group_at(iota((PG, PG), 0)) == iota((PG, PG), 1)).astype(F32)
    cols_ref[...] = dot(order, local, NT, EXACT)
    first_ref[...] = dot(order, start_ref[...], NT, EXACT)
    twice = jnp.broadcast_to(cols_ref[:, 2:3] * 2.0, (PG, C))
    pre_ref[0] = twice
    pre_ref[1] = twice * jax.nn.sigmoid(LAPSE_SLOPE * (rates[0:1] - first_ref[...]))
    pre_ref[2] = first_ref[...]

    gathered = jnp.concatenate(powers[2] + [powers[1][0], powers[0][0], stays[1], stays[0]], axis=0)
    gathered = stack_parts(gathered, 2, 192)
    for tile in range(M // TILE):
        at = pl.ds(tile * TILE, TILE)
        found = dot(gathered, point_ref[:, at], NN)
        found = found[0:96] + found[96:192]
        states = state_ref[:, at]
        last = jnp.zeros((S, TILE), F32)
        for s in range(S):
            last = jnp.where(states == s, found[s * S : (s + 1) * S], last)
        held = iota((S, TILE), 0) == states
        second = jnp.sum(jnp.where(held, found[80:88], 0.0), axis=0, keepdims=True)
        first = jnp.sum(jnp.where(held, found[88:96], 0.0), axis=0, keepdims=True)
        start = (states == 0).astype(F32)
        table_ref[0:8, at] = last
        table_ref[8:16, at] = found[0:8]
        table_ref[16:24, at] = found[64:72]
        table_ref[24:32, at] = found[72:80]
        table_ref[32:40, at] = jnp.concatenate(
            [start, first, second, account_ref[:, at], jnp.zeros((4, TILE), F32)], axis=0
        )

    from_mp(lambda peer: b_src.at[pair(peer)], lambda peer: b_buf.at[peer], b_send, b_recv, mp_peers, lambda peer: peer)
    total = b_buf[0]
    for slot in range(1, MP):
        total = total + b_buf[slot]
    rows = pl.ds(pl.multiple_of(sc * KD, KD), KD)
    c_buf[rows, :] = total
    copies = to_scen(c_buf.at[rows, :], c_buf.at[rows, :], c_send, c_recv)
    for copy in copies:
        copy.start()
    sends += copies

    from_mp(lambda peer: e_src.at[pair(peer)], lambda peer: e_buf.at[peer], e_send, e_recv, mp_peers, lambda peer: peer)
    early = e_buf[0]
    for slot in range(1, MP):
        early = early + e_buf[slot]
    early = jnp.transpose(jnp.concatenate([early, jnp.zeros((C - 8, C), F32)], axis=0))
    income = early[GQ : 2 * GQ]
    mine = pl.ds(pl.multiple_of(own * GQ, GQ), GQ)
    columns = cols_ref[mine, :]
    guarantee, spread, lapse_base = columns[:, 0:1], columns[:, 1:2], columns[:, 2:3]
    stay = [columns[:, 3:4], columns[:, 4:5]]
    pay = [columns[:, 5:6], columns[:, 6:7], columns[:, 7:8]]
    credited = first_ref[mine, :]

    def rows_at(peer):
        return pl.ds(pl.multiple_of(peer * KD, KD), KD)

    from_scen(c_buf.at[rows, :], lambda peer: c_buf.at[rows_at(peer), :], c_send, c_recv)
    worth = jnp.transpose(c_buf[...])
    assets = []
    for date in range(DATES):
        pieces = stack_parts(worth[date * GQ : (date + 1) * GQ], 3, 3 * GQ)
        high = dot(pieces, disc_ref[date, 0], NN)
        middle = dot(pieces[: 2 * GQ], disc_ref[date, 1], NN)
        low = dot(pieces[:GQ], disc_ref[date, 2], NN)
        assets.append(
            high[:GQ] + ((high[GQ : 2 * GQ] + middle[:GQ]) + (high[2 * GQ :] + middle[GQ:] + low))
        )

    growth = jnp.ones((GQ, C), F32)
    present = jnp.zeros((GQ, C), F32)
    lapses = []
    for month in range(MONTHS):
        factor = lapse_base * 2.0 * jax.nn.sigmoid(LAPSE_SLOPE * (rates[month : month + 1] - credited))
        mass = early[:GQ, month : month + 1]
        for lag, lapse in enumerate(reversed(lapses)):
            mass = mass - lapse * stay[lag]
        lapses.append(mass * factor)
        growth = growth * (1.0 + credited / 12.0)
        paid = early[:GQ, 3 + month : 4 + month]
        for lag, lapse in enumerate(reversed(lapses)):
            paid = paid - lapse * pay[lag]
        flows = growth * (lapses[-1] + paid)
        held = assets[month]
        later = assets[month + 1] + income[:, month : month + 1]
        earned = 12.0 * (later - held) / held
        credited = jnp.maximum(
            guarantee, 0.5 * credited + 0.5 * (earned - spread) - LIQUID_CHARGE * flows / held
        )
        if month < MONTHS - 1:
            d_buf[mine, month * C : (month + 1) * C] = credited
        present = present + flows * jnp.exp(-rates[month + 1 : month + 2] * ((month + 1) / 12.0))
    d_copies = to_mp(lambda peer: d_buf.at[mine, :], d_buf.at[mine, :], d_send, d_recv, near_peers, own)
    for copy in d_copies:
        copy.start()
    half = jnp.where(zh == 0, present[:16], present[16:])
    f_src[...] = dot(jnp.ones((8, C), F32), jnp.concatenate([half, jnp.zeros((C - 16, C), F32)], axis=0), NT, EXACT)
    f_copies = to_scen(f_src, f_buf.at[sc], f_send, f_recv)
    for copy in f_copies:
        copy.start()
    sends += d_copies + f_copies
    f_buf[sc] = f_src[...]
    credited_ref[...] = 100.0 * jnp.where(zh == 0, credited[:16], credited[16:])

    def pair_rows(peer):
        return pl.ds(pl.multiple_of(pair(peer) * GQ, GQ), GQ)

    from_mp(lambda peer: d_buf.at[mine, :], lambda peer: d_buf.at[pair_rows(peer), :], d_send, d_recv, near_peers, pair)
    rho_ref[...] = d_buf[...]
    from_scen(f_src, lambda peer: f_buf.at[peer], f_send, f_recv)
    value = f_buf[0]
    for slot in range(1, SC):
        value = value + f_buf[slot]
    value_ref[...] = value * (1.0 / SCEN)
    for copy in sends:
        copy.wait_send()


CHUNK = 32


def output_kernel(
    group_ref, path_ref, rho_ref, pre_ref, table_ref, credited_in, value_in,
    occupancy_hbm, account_hbm, credited_ref, value_ref,
    point_ref, occupancy_ref, account_ref, sems,
):
    credited_ref[...] = credited_in[...]
    value_ref[...] = value_in[0:1, 0:16]
    labels = group_at(iota((PG, TILE), 0))
    for tile in range(M // TILE):
        at = pl.ds(tile * TILE, TILE)
        point_ref[:, at] = (labels == group_ref[:, at]).astype(BF16)
    twice = pre_ref[0]
    rho = [pre_ref[2], rho_ref[:, :C], rho_ref[:, C:]]
    tables = [pre_ref[1]]
    for month in (1, 2):
        tables.append(twice * jax.nn.sigmoid(LAPSE_SLOPE * (path_ref[month : month + 1, :] - rho[month])))
    grown = [rate / 12.0 for rate in rho]
    gain = grown[0] + grown[1] + grown[0] * grown[1]
    tables.append(gain + grown[2] + gain * grown[2])
    tables = [parts(jnp.transpose(table), 2) for table in tables]

    copies = []
    for chunk in range(C // CHUNK):
        rows = slice(chunk * CHUNK, (chunk + 1) * CHUNK)
        lhs = jnp.concatenate([piece[rows] for table in tables for piece in table], axis=0)
        for tile in range(M // TILE):
            at = pl.ds(tile * TILE, TILE)
            found = dot(lhs, point_ref[:, at], NN)
            found = [
                found[2 * n * CHUNK : (2 * n + 1) * CHUNK] + found[(2 * n + 1) * CHUNK : (2 * n + 2) * CHUNK]
                for n in range(4)
            ]
            first = found[0] * table_ref[32:33, at]
            second = (table_ref[33:34, at] - first * table_ref[24:25, at]) * found[1]
            third = (table_ref[34:35, at] - first * table_ref[16:17, at] - second * table_ref[24:25, at]) * found[2]
            for u in range(S):
                occupancy_ref[u, rows, at] = (
                    table_ref[u : u + 1, at]
                    - first * table_ref[8 + u : 9 + u, at]
                    - second * table_ref[16 + u : 17 + u, at]
                    - third * table_ref[24 + u : 25 + u, at]
                )
            account = table_ref[35:36, at]
            account_ref[rows, at] = account + account * found[3]
        copies.append(pltpu.make_async_copy(occupancy_ref.at[:, rows, :], occupancy_hbm.at[:, rows, :], sems.at[0, chunk]))
        copies.append(pltpu.make_async_copy(account_ref.at[rows, :], account_hbm.at[rows, :], sems.at[1, chunk]))
        copies[-2].start()
        copies[-1].start()
    for copy in copies:
        copy.wait()


def vmem(*shape):
    return pltpu.VMEM(shape, F32)


def body(
    group_id,
    issue_state,
    account_start,
    transition,
    lapse_base,
    benefit,
    bond_block,
    bond_flows,
    bond_target,
    base_rate,
    rate_moves,
    guarantee,
    spread,
    start_rate,
):
    in_vmem = pl.BlockSpec(memory_space=pltpu.VMEM)
    in_smem = pl.BlockSpec(memory_space=pltpu.SMEM)
    anywhere = pl.BlockSpec(memory_space=pl.ANY)
    groups = group_id.reshape(1, M)
    dma = pltpu.SemaphoreType.DMA
    rho, pre, table, credited, value, path = pl.pallas_call(
        exchange_kernel,
        out_shape=[
            jax.ShapeDtypeStruct((PG, 2 * C), F32),
            jax.ShapeDtypeStruct((3, PG, C), F32),
            jax.ShapeDtypeStruct((40, M), F32),
            jax.ShapeDtypeStruct((16, C), F32),
            jax.ShapeDtypeStruct((8, C), F32),
            jax.ShapeDtypeStruct((8, C), F32),
        ],
        in_specs=[in_vmem] * 5 + [in_smem, in_vmem, anywhere] + [in_vmem] * 4,
        out_specs=[in_vmem] * 6,
        scratch_shapes=[
            vmem(B, K),
            pltpu.VMEM((3, B, K), BF16),
            vmem(KD, B),
            pltpu.VMEM((PG, B), BF16),
            pltpu.VMEM((PG, M), BF16),
            pltpu.VMEM((DATES, 3, K, C), BF16),
            vmem(PG, 8),
            vmem(PG, C),
            vmem(8, C),
            vmem(SC, 8, C),
            vmem(MP // 2, 8, C),
            vmem(MP, 8, C),
            vmem(MP // 2, KD, C),
            vmem(MP, KD, C),
            vmem(K, C),
            vmem(PG, 2 * C),
            vmem(8, C),
            vmem(SC, 8, C),
            dma,
            dma((SC,)), dma((SC,)),
            dma((MP,)), dma((MP,)),
            dma((MP,)), dma((MP,)),
            dma((SC,)), dma((SC,)),
            dma((MP,)), dma((MP,)),
            dma((SC,)), dma((SC,)),
        ],
        compiler_params=pltpu.CompilerParams(
            collective_id=0, has_side_effects=True, vmem_limit_bytes=VMEM_LIMIT
        ),
        name="exchange",
    )(
        groups,
        issue_state.reshape(1, M),
        account_start.reshape(1, M),
        transition.transpose(1, 2, 0),
        jnp.stack([guarantee, spread, lapse_base]),
        benefit,
        bond_block.reshape(1, B),
        bond_flows,
        bond_target.reshape(1, B),
        base_rate.reshape(1, C),
        rate_moves,
        start_rate,
    )
    occupancy, account_value, credited, value = pl.pallas_call(
        output_kernel,
        out_shape=[
            jax.ShapeDtypeStruct((S, C, M), F32),
            jax.ShapeDtypeStruct((C, M), F32),
            jax.ShapeDtypeStruct((16, C), F32),
            jax.ShapeDtypeStruct((1, 16), F32),
        ],
        in_specs=[in_vmem] * 7,
        out_specs=[anywhere, anywhere, in_vmem, in_vmem],
        scratch_shapes=[pltpu.VMEM((PG, M), BF16), vmem(S, C, M), vmem(C, M), dma((2, C // CHUNK))],
        compiler_params=pltpu.CompilerParams(vmem_limit_bytes=VMEM_LIMIT),
        name="outputs",
    )(groups, path, rho, pre, table, credited, value)
    return occupancy, account_value, credited.T, value.reshape(16)


def solution(mesh):
    placed = (
        P("mp"),
        P("mp"),
        P("mp"),
        P(),
        P(),
        P(),
        P("mp", None),
        P("mp", None),
        P("mp"),
        P("scen"),
        P(None, "scen"),
        P(),
        P(),
        P("scen", None),
    )
    return jax.shard_map(
        body,
        mesh=mesh,
        in_specs=placed,
        out_specs=(P(None, "scen", "mp"), P("scen", "mp"), P("scen", "mp"), P("mp")),
        check_vma=False,
    )
```

```python
import functools

import jax
import jax.numpy as jnp
from jax import lax
from jax.experimental import pallas as pl
from jax.experimental.pallas import tpu as pltpu
from jax.sharding import PartitionSpec as P

MESH = pl.DeviceIdType.MESH
EXACT = lax.Precision.HIGHEST
F32, BF16 = jnp.float32, jnp.bfloat16
STAY_WEIGHT = 40.0
LAPSE_SLOPE = 30.0
LIQUID_CHARGE = 0.5

S = 8
PG = 256
K = 256
DATES = 4
MONTHS = 3
C = 128
M = 1024
B = 2560
TILE = 256
MP = 16
SC = 16
SCEN = C * SC
KD = K // SC
GQ = 2 * PG // MP
VMEM_LIMIT = 56 * 1024 * 1024

NT = (((1,), (1,)), ((), ()))
NN = (((1,), (0,)), ((), ()))


def dot(a, b, dims, precision=None):
    return lax.dot_general(a, b, dims, precision=precision, preferred_element_type=F32)


def parts(x, count):
    found = []
    for _ in range(count):
        found.append(x.astype(BF16))
        x = x - found[-1].astype(F32)
    return found


def stack_parts(x, count, rows):
    found = parts(x, count)
    pieces = [piece.astype(F32) for piece in found]
    rest = rows - count * x.shape[0]
    if rest:
        pieces.append(jnp.zeros((rest, x.shape[1]), F32))
    return jnp.concatenate(pieces, axis=0).astype(BF16)


def iota(shape, axis):
    return lax.broadcasted_iota(jnp.int32, shape, axis)


def group_at(place):
    block = place // 16
    return (block // 4 * 4 + block % 2 * 2 + block // 2 % 2) * 16 + place % 16


def swap_blocks(rows):
    block = iota(rows.shape, 1) // 16 % 4
    width = rows.shape[1]
    up = pltpu.roll(rows, width - 16, 1)
    down = pltpu.roll(rows, 16, 1)
    return jnp.where(block == 1, up, jnp.where(block == 2, down, rows))


def discounts(rates, date):
    horizon = iota((K, C), 0)
    tenor = (horizon - date + 1).astype(F32) / 12.0
    factor = jnp.exp(-tenor * rates[date : date + 1, :])
    return jnp.where(horizon >= date, factor, 0.0) if date else factor


def exchange_kernel(
    base_hbm,
    moves_hbm,
    block_hbm,
    flows_hbm,
    group_hbm,
    state_hbm,
    account_hbm,
    transition_hbm,
    benefit_hbm,
    guarantee_hbm,
    spread_hbm,
    lapse_hbm,
    target_hbm,
    start_hbm,
    rho_hbm,
    pre_hbm,
    table_hbm,
    lapse1_hbm,
    point_hbm,
    small_hbm,
    value_hbm,
    pre_ref,
    table_ref,
    lapse1_ref,
    point_ref,
    small_ref,
    base_ref,
    moves_ref,
    block_ref,
    flows_ref,
    group_ref,
    state_ref,
    account_ref,
    transition_ref,
    benefit_ref,
    guarantee_ref,
    spread_ref,
    lapse_ref,
    target_ref,
    start_ref,
    flow_parts,
    chosen_ref,
    bond_ref,
    disc_ref,
    cols_ref,
    first_ref,
    a_src,
    a_buf,
    e_src,
    e_buf,
    b_src,
    b_buf,
    c_buf,
    d_src,
    f_src,
    load_sem,
    store_sem,
    a_send,
    a_recv,
    e_send,
    e_recv,
    b_send,
    b_recv,
    c_send,
    c_recv,
    d_send,
    d_recv,
    f_send,
    f_recv,
):
    mp, sc = lax.axis_index("mp"), lax.axis_index("scen")
    x, zh, core = mp // 4, mp // 2 % 2, mp % 2
    own = x * 2 + core
    zl, y = sc // 4, sc % 4

    def mp_index(dx, dz, dc):
        return (x + dx) % 4 * 4 + (zh + dz) % 2 * 2 + (core + dc) % 2

    def months_of(scen, half):
        return (scen // 4 + 2 * half) % 4 * 4 + scen % 4

    def scen_peer(dz, dy):
        there = (zl + dz) % 4
        across = (there - zl) * (there - zl) // 9
        return mp_index(0, across, 0), there * 4 + (y + dy) % 4

    steps = [(dz, dy) for dz in (2, 1, 3, 0) for dy in (2, 1, 3, 0) if (dz, dy) != (0, 0)]
    a_peers = [scen_peer(dz, dy) for dz, dy in steps]
    c_peers = [(mp, (zl + dz) % 4 * 4 + (y + dy) % 4) for dz, dy in steps]
    b_peers = [
        (mp_index(dx, dz, dc), (zl + 2 * dz) % 4 * 4 + y)
        for dz in (1, 0)
        for dx in (2, 1, 3, 0)
        for dc in (0, 1)
        if (dx, dz, dc) != (0, 0, 0)
    ]
    d_peers = [(mp_index(dx, 0, dc), sc) for dx in (2, 1, 3, 0) for dc in (0, 1) if (dx, dc) != (0, 0)]

    barrier = pltpu.get_barrier_semaphore()
    for peer in a_peers + b_peers + c_peers:
        pl.semaphore_signal(barrier, inc=1, device_id=peer, device_id_type=MESH)
    loads = [
        pltpu.make_async_copy(src, dst, load_sem.at[n])
        for n, (src, dst) in enumerate(
            [
                (base_hbm, base_ref),
                (moves_hbm, moves_ref),
                (block_hbm, block_ref),
                (flows_hbm, flows_ref),
                (group_hbm, group_ref),
                (state_hbm, state_ref),
                (account_hbm, account_ref),
                (transition_hbm, transition_ref),
                (benefit_hbm, benefit_ref),
                (guarantee_hbm, guarantee_ref),
                (spread_hbm, spread_ref),
                (lapse_hbm, lapse_ref),
                (target_hbm, target_ref),
                (start_hbm, start_ref),
            ]
        )
    ]
    for load in loads:
        load.start()

    def send_to(peers, src, dst, sems, mark):
        copies = [
            pltpu.make_async_remote_copy(
                src_ref=src(peer), dst_ref=dst, send_sem=sems[0].at[n], recv_sem=sems[1].at[mark],
                device_id=peer, device_id_type=MESH,
            )
            for n, peer in enumerate(peers)
        ]
        for copy in copies:
            copy.start()
        return copies

    def wait_from(peers, src, slot, sems, mark):
        for n, peer in enumerate(peers):
            pltpu.make_async_remote_copy(
                src_ref=src(peer), dst_ref=slot(peer), send_sem=sems[0].at[n], recv_sem=sems[1].at[mark(peer)],
                device_id=peer, device_id_type=MESH,
            ).wait_recv()

    def pair(peer):
        return peer[0] // 4 * 2 + peer[0] % 2

    a_sems, b_sems, c_sems = (a_send, a_recv), (b_send, b_recv), (c_send, c_recv)
    d_sems, e_sems, f_sems = (d_send, d_recv), (e_send, e_recv), (f_send, f_recv)
    months = months_of(sc, zh)

    for load in loads[:2]:
        load.wait()
    rates = [base_ref[...]]
    for month in range(MONTHS):
        rates.append(rates[-1] + moves_ref[month : month + 1, :])
    rates = jnp.concatenate(rates, axis=0)
    blank = jnp.zeros((8, C), F32)
    small_ref[16:32, :] = jnp.concatenate([blank, rates, blank[:4]], axis=0)
    ones = jnp.ones((16, C), BF16)
    sums = []
    for date in range(DATES):
        pieces = parts(discounts(rates, date), 3)
        total = jnp.zeros((16, K), F32)
        for number, piece in enumerate(pieces):
            disc_ref[date, number] = piece
        for piece in reversed(pieces):
            total = total + dot(ones, piece, NT)
        sums.append(total[0:1])
    sums = jnp.concatenate(sums, axis=0)
    a_src[...] = jnp.concatenate([sums[:, : K // 2], sums[:, K // 2 :]], axis=0)

    pl.semaphore_wait(barrier, len(a_peers + b_peers + c_peers))
    sends = send_to(a_peers, lambda peer: a_src, a_buf.at[sc], a_sems, sc)
    a_buf[sc] = a_src[...]

    for load in loads[2:4]:
        load.wait()
    picks = iota((32, K), 0)
    wanted = jnp.where(picks < KD, months * KD + picks, picks - KD)
    chosen = ((iota((32, K), 1) == wanted) & (picks < KD + MONTHS)).astype(BF16)
    bond_labels = group_at(iota((PG, TILE), 0))

    def prepare(tile, income):
        at = pl.ds(pl.multiple_of(tile * TILE, TILE), TILE)
        pieces = parts(flows_ref[at, :], 3)
        for number, piece in enumerate(pieces):
            flow_parts[number, at, :] = piece
        found = dot(chosen, pieces[2], NT) + dot(chosen, pieces[1], NT) + dot(chosen, pieces[0], NT)
        chosen_ref[:, at] = found[:KD]
        groups = (bond_labels == block_ref[:, at]).astype(BF16)
        bond_ref[:, at] = groups
        return income + dot(stack_parts(found[KD : KD + 8], 3, 32), groups, NT)

    income = lax.fori_loop(0, B // TILE, prepare, jnp.zeros((32, PG), F32))
    income = income[0:8] + income[8:16] + income[16:24]

    for load in loads[4:]:
        load.wait()
    accounts = jnp.zeros((32, PG), F32)
    for tile in range(M // TILE):
        at = pl.ds(tile * TILE, TILE)
        groups = (bond_labels == group_ref[:, at]).astype(BF16)
        point_ref[:, at] = groups
        mass = jnp.where(iota((S, TILE), 0) == state_ref[:, at], account_ref[:, at], 0.0)
        accounts = accounts + dot(stack_parts(mass, 3, 32), groups, NT)
    accounts = accounts[0:8] + accounts[8:16] + accounts[16:24]

    move = []
    for s in range(S):
        row = transition_ref[s] + jnp.where(iota((S, PG), 0) == s, STAY_WEIGHT, 0.0)
        move.append(row / jnp.sum(row, axis=0, keepdims=True))
    powers = [move]
    for _ in range(MONTHS - 1):
        last = powers[-1]
        powers.append([functools.reduce(jnp.add, [last[s][v : v + 1] * move[v] for v in range(S)]) for s in range(S)])
    benefit = jnp.where(iota((S, S), 0) == iota((S, S), 1), benefit_ref[...], 0.0)
    benefit = jnp.sum(benefit, axis=1, keepdims=True)
    stays = [jnp.concatenate([power[s][0:1] for s in range(S)], axis=0) for power in powers]
    pays = [
        jnp.concatenate([jnp.sum(power[s] * benefit, axis=0, keepdims=True) for s in range(S)], axis=0)
        for power in powers
    ]

    def by_state(rows):
        return jnp.sum(accounts * swap_blocks(rows), axis=0, keepdims=True)

    early = [accounts[0:1], by_state(stays[0]), by_state(stays[1]), by_state(pays[0]), by_state(pays[1]), by_state(pays[2])]
    early = jnp.concatenate(early + [jnp.zeros((2, PG), F32)], axis=0)
    for q in range(MP // 2):
        e_src[q] = jnp.concatenate(
            [early[:, q * GQ : (q + 1) * GQ], income[:, q * GQ : (q + 1) * GQ], jnp.zeros((8, C - 2 * GQ), F32)], axis=1
        )
    sends += send_to(b_peers, lambda peer: e_src.at[pair(peer)], e_buf.at[mp], e_sems, mp)
    e_buf[mp] = e_src[own]

    wait_from(a_peers, lambda peer: a_src, lambda peer: a_buf.at[peer[1]], a_sems, lambda peer: peer[1])
    mean = a_buf[0]
    for slot in range(1, SC):
        mean = mean + a_buf[slot]
    mean = mean * (1.0 / SCEN)
    mean = stack_parts(jnp.concatenate([mean[0:4], mean[4:8]], axis=1), 3, 16)

    def weigh(tile, total):
        at = pl.ds(pl.multiple_of(tile * TILE, TILE), TILE)
        high = dot(mean, flow_parts[0, at, :], NT)
        middle = dot(mean, flow_parts[1, at, :], NT)
        low = dot(mean, flow_parts[2, at, :], NT)
        price = high[0:4] + ((high[4:8] + middle[0:4]) + (high[8:12] + middle[4:8] + low[0:4]))
        target = [target_ref[pl.ds(tile * 2 + n, 1), :] for n in range(2)]
        weight = jnp.concatenate(target, axis=1) / price
        flows = chosen_ref[:, at]
        scaled = jnp.concatenate([weight[date : date + 1] * flows for date in range(DATES)], axis=0)
        return total + dot(stack_parts(scaled, 3, 3 * DATES * KD), bond_ref[:, at], NT)

    worth = lax.fori_loop(0, B // TILE, weigh, jnp.zeros((3 * DATES * KD, PG), F32), unroll=True)
    size = DATES * KD
    worth = worth[0:size] + (worth[size : 2 * size] + worth[2 * size :])
    for q in range(MP // 2):
        b_src[q] = jnp.concatenate(
            [worth[date * KD : (date + 1) * KD, q * GQ : (q + 1) * GQ] for date in range(DATES)], axis=1
        )
    sends += send_to(b_peers, lambda peer: b_src.at[pair(peer)], b_buf.at[mp], b_sems, mp)
    b_buf[mp] = b_src[own]

    local = [guarantee_ref[...], spread_ref[...], lapse_ref[...], stays[0][0:1], stays[1][0:1], pays[0][0:1], pays[1][0:1], pays[2][0:1]]
    local = jnp.concatenate(local, axis=0)
    order = (group_at(iota((PG, PG), 0)) == iota((PG, PG), 1)).astype(F32)
    cols_ref[...] = dot(order, local, NT, EXACT)
    first_ref[...] = dot(order, start_ref[...], NT, EXACT)
    twice = jnp.broadcast_to(cols_ref[:, 2:3] * 2.0, (PG, C))
    pre_ref[0] = twice
    pre_ref[1] = first_ref[...]
    start_lapse = twice * jax.nn.sigmoid(LAPSE_SLOPE * (rates[0:1] - first_ref[...]))
    start_lapse = stack_parts(jnp.transpose(start_lapse), 2, 2 * C)

    gathered = jnp.concatenate(powers[2] + [powers[1][0], powers[0][0], stays[1], stays[0]], axis=0)
    gathered = stack_parts(swap_blocks(gathered), 2, 192)
    for tile in range(M // TILE):
        at = pl.ds(tile * TILE, TILE)
        found = dot(gathered, point_ref[:, at], NN)
        found = found[0:96] + found[96:192]
        states = state_ref[:, at]
        last = jnp.zeros((S, TILE), F32)
        for s in range(S):
            last = jnp.where(states == s, found[s * S : (s + 1) * S], last)
        held = iota((S, TILE), 0) == states
        second = jnp.sum(jnp.where(held, found[80:88], 0.0), axis=0, keepdims=True)
        first = jnp.sum(jnp.where(held, found[88:96], 0.0), axis=0, keepdims=True)
        start = (states == 0).astype(F32)
        lapsed = dot(start_lapse, point_ref[:, at], NN)
        lapse1_ref[:, at] = (lapsed[:C] + lapsed[C:]) * start
        table_ref[0:8, at] = last
        table_ref[8:16, at] = found[0:8]
        table_ref[16:24, at] = found[64:72]
        table_ref[24:32, at] = found[72:80]
        table_ref[32:40, at] = jnp.concatenate(
            [start, first, second, account_ref[:, at], jnp.zeros((4, TILE), F32)], axis=0
        )
    stores = [
        pltpu.make_async_copy(src, dst, store_sem.at[n])
        for n, (src, dst) in enumerate(
            [
                (pre_ref, pre_hbm),
                (table_ref, table_hbm),
                (lapse1_ref, lapse1_hbm),
                (point_ref, point_hbm),
                (small_ref, small_hbm),
            ]
        )
    ]
    for store in stores[:4]:
        store.start()

    wait_from(
        b_peers, lambda peer: b_src.at[pair(peer)], lambda peer: b_buf.at[peer[0]], b_sems, lambda peer: peer[0]
    )
    total = b_buf[0]
    for slot in range(1, MP):
        total = total + b_buf[slot]
    rows = pl.ds(pl.multiple_of(months * KD, KD), KD)
    c_buf[rows, :] = total
    sends += send_to(c_peers, lambda peer: c_buf.at[rows, :], c_buf.at[rows, :], c_sems, sc)

    wait_from(
        b_peers, lambda peer: e_src.at[pair(peer)], lambda peer: e_buf.at[peer[0]], e_sems, lambda peer: peer[0]
    )
    early = e_buf[0]
    for slot in range(1, MP):
        early = early + e_buf[slot]
    early = jnp.transpose(jnp.concatenate([early, jnp.zeros((C - 8, C), F32)], axis=0))
    income = early[GQ : 2 * GQ]
    mine = pl.ds(pl.multiple_of(own * GQ, GQ), GQ)
    columns = cols_ref[mine, :]
    guarantee, spread, lapse_base = columns[:, 0:1], columns[:, 1:2], columns[:, 2:3]
    stay = [columns[:, 3:4], columns[:, 4:5]]
    pay = [columns[:, 5:6], columns[:, 6:7], columns[:, 7:8]]
    credited = first_ref[mine, :]

    def rows_at(peer):
        return pl.ds(pl.multiple_of(months_of(peer[1], zh) * KD, KD), KD)

    wait_from(
        c_peers, lambda peer: c_buf.at[rows, :], lambda peer: c_buf.at[rows_at(peer), :], c_sems, lambda peer: peer[1]
    )
    worth = jnp.transpose(c_buf[...])
    assets = []
    for date in range(DATES):
        pieces = stack_parts(worth[date * GQ : (date + 1) * GQ], 3, 3 * GQ)
        high = dot(pieces, disc_ref[date, 0], NN)
        middle = dot(pieces[: 2 * GQ], disc_ref[date, 1], NN)
        low = dot(pieces[:GQ], disc_ref[date, 2], NN)
        assets.append(
            high[:GQ] + ((high[GQ : 2 * GQ] + middle[:GQ]) + (high[2 * GQ :] + middle[GQ:] + low))
        )

    growth = jnp.ones((GQ, C), F32)
    present = jnp.zeros((GQ, C), F32)
    lapses = []
    for month in range(MONTHS):
        factor = lapse_base * 2.0 * jax.nn.sigmoid(LAPSE_SLOPE * (rates[month : month + 1] - credited))
        mass = early[:GQ, month : month + 1]
        for lag, lapse in enumerate(reversed(lapses)):
            mass = mass - lapse * stay[lag]
        lapses.append(mass * factor)
        growth = growth * (1.0 + credited / 12.0)
        paid = early[:GQ, 3 + month : 4 + month]
        for lag, lapse in enumerate(reversed(lapses)):
            paid = paid - lapse * pay[lag]
        flows = growth * (lapses[-1] + paid)
        held = assets[month]
        later = assets[month + 1] + income[:, month : month + 1]
        earned = 12.0 * (later - held) / held
        credited = jnp.maximum(
            guarantee, 0.5 * credited + 0.5 * (earned - spread) - LIQUID_CHARGE * flows / held
        )
        if month < MONTHS - 1:
            d_src[:, month * C : (month + 1) * C] = credited
        present = present + flows * jnp.exp(-rates[month + 1 : month + 2] * ((month + 1) / 12.0))
    sends += send_to(d_peers, lambda peer: d_src, rho_hbm.at[mine, :], d_sems, own)
    stores.append(pltpu.make_async_copy(d_src, rho_hbm.at[mine, :], store_sem.at[5]))
    stores[5].start()
    sums = dot(jnp.ones((8, C), F32), jnp.concatenate([present, jnp.zeros((C - GQ, C), F32)], axis=0), NT, EXACT)
    f_src[0] = sums
    f_src[1] = pltpu.roll(sums, C - 16, 1)
    sends += send_to(a_peers, lambda peer: f_src.at[peer[0] // 2 % 2], value_hbm.at[sc], f_sems, sc)
    stores.append(pltpu.make_async_copy(f_src.at[zh], value_hbm.at[sc], store_sem.at[6]))
    stores[6].start()
    small_ref[0:16, :] = 100.0 * jnp.where(zh == 0, credited[:16], credited[16:])
    stores[4].start()

    def pair_rows(peer):
        return pl.ds(pl.multiple_of(pair(peer) * GQ, GQ), GQ)

    wait_from(d_peers, lambda peer: d_src, lambda peer: rho_hbm.at[pair_rows(peer), :], d_sems, pair)
    wait_from(
        a_peers, lambda peer: f_src.at[peer[0] // 2 % 2], lambda peer: value_hbm.at[peer[1]], f_sems, lambda peer: peer[1]
    )
    for store in stores:
        store.wait()
    for copy in sends:
        copy.wait_send()


CHUNK = 32


def output_kernel(
    rho_hbm, pre_hbm, table_hbm, lapse1_hbm, point_hbm, small_hbm, value_hbm,
    occupancy_hbm, account_hbm, credited_ref, value_ref,
    rho_ref, pre_ref, table_ref, lapse1_ref, point_ref, small_ref, sums_ref,
    occupancy_ref, account_ref, load_sem, store_sem,
):
    loads = [
        pltpu.make_async_copy(src, dst, load_sem.at[n])
        for n, (src, dst) in enumerate(
            [
                (rho_hbm, rho_ref),
                (pre_hbm, pre_ref),
                (small_hbm, small_ref),
                (point_hbm, point_ref),
                (table_hbm, table_ref),
                (lapse1_hbm, lapse1_ref),
                (value_hbm, sums_ref),
            ]
        )
    ]
    for load in loads:
        load.start()
    for load in loads[:3]:
        load.wait()
    credited_ref[...] = small_ref[0:16, :]
    twice = pre_ref[0]
    rho = [pre_ref[1], rho_ref[:, :C], rho_ref[:, C:]]
    tables = []
    for month in (1, 2):
        rates = small_ref[24 + month : 25 + month, :]
        tables.append(twice * jax.nn.sigmoid(LAPSE_SLOPE * (rates - rho[month])))
    grown = [rate * (1.0 / 12.0) for rate in rho]
    gain = grown[0] + grown[1] + grown[0] * grown[1]
    tables.append(gain + grown[2] + gain * grown[2])
    tables = [parts(jnp.transpose(table), 2) for table in tables]

    for load in loads[3:]:
        load.wait()
    value = sums_ref[0]
    for slot in range(1, SC):
        value = value + sums_ref[slot]
    value_ref[...] = value[0:1, 0:16] * (1.0 / SCEN)
    copies = []
    for chunk in range(C // CHUNK):
        rows = slice(chunk * CHUNK, (chunk + 1) * CHUNK)
        lhs = jnp.concatenate([piece[rows] for table in tables for piece in table], axis=0)
        for tile in range(M // TILE):
            at = pl.ds(tile * TILE, TILE)
            found = dot(lhs, point_ref[:, at], NN)
            found = [
                found[2 * n * CHUNK : (2 * n + 1) * CHUNK] + found[(2 * n + 1) * CHUNK : (2 * n + 2) * CHUNK]
                for n in range(3)
            ]
            first = lapse1_ref[rows, at]
            second = (table_ref[33:34, at] - first * table_ref[24:25, at]) * found[0]
            third = (table_ref[34:35, at] - first * table_ref[16:17, at] - second * table_ref[24:25, at]) * found[1]
            for u in range(S):
                occupancy_ref[u, rows, at] = (
                    table_ref[u : u + 1, at]
                    - first * table_ref[8 + u : 9 + u, at]
                    - second * table_ref[16 + u : 17 + u, at]
                    - third * table_ref[24 + u : 25 + u, at]
                )
            account = table_ref[35:36, at]
            account_ref[rows, at] = account + account * found[2]
        copies.append(
            pltpu.make_async_copy(occupancy_ref.at[:, rows, :], occupancy_hbm.at[:, rows, :], store_sem.at[0, chunk])
        )
        copies.append(pltpu.make_async_copy(account_ref.at[rows, :], account_hbm.at[rows, :], store_sem.at[1, chunk]))
        copies[-2].start()
        copies[-1].start()
    for copy in copies:
        copy.wait()


def vmem(*shape):
    return pltpu.VMEM(shape, F32)


def body(
    group_id,
    issue_state,
    account_start,
    transition,
    lapse_base,
    benefit,
    bond_block,
    bond_flows,
    bond_target,
    base_rate,
    rate_moves,
    guarantee,
    spread,
    start_rate,
):
    in_vmem = pl.BlockSpec(memory_space=pltpu.VMEM)
    in_hbm = pl.BlockSpec(memory_space=pltpu.HBM)
    dma = pltpu.SemaphoreType.DMA
    between = pl.pallas_call(
        exchange_kernel,
        out_shape=[
            jax.ShapeDtypeStruct((PG, 2 * C), F32),
            jax.ShapeDtypeStruct((2, PG, C), F32),
            jax.ShapeDtypeStruct((40, M), F32),
            jax.ShapeDtypeStruct((C, M), F32),
            jax.ShapeDtypeStruct((PG, M), BF16),
            jax.ShapeDtypeStruct((32, C), F32),
            jax.ShapeDtypeStruct((SC, 8, C), F32),
        ],
        in_specs=[in_hbm] * 14,
        out_specs=[in_hbm] * 7,
        scratch_shapes=[
            vmem(2, PG, C),
            vmem(40, M),
            vmem(C, M),
            pltpu.VMEM((PG, M), BF16),
            vmem(32, C),
            vmem(1, C),
            vmem(MONTHS, C),
            pltpu.VMEM((1, B), jnp.int32),
            vmem(B, K),
            pltpu.VMEM((1, M), jnp.int32),
            pltpu.VMEM((1, M), jnp.int32),
            vmem(1, M),
            vmem(S, S, PG),
            vmem(1, S),
            vmem(1, PG),
            vmem(1, PG),
            vmem(1, PG),
            vmem(B // C, C),
            vmem(C, PG),
            pltpu.VMEM((3, B, K), BF16),
            vmem(KD, B),
            pltpu.VMEM((PG, B), BF16),
            pltpu.VMEM((DATES, 3, K, C), BF16),
            vmem(PG, 8),
            vmem(PG, C),
            vmem(8, C),
            vmem(SC, 8, C),
            vmem(MP // 2, 8, C),
            vmem(MP, 8, C),
            vmem(MP // 2, KD, C),
            vmem(MP, KD, C),
            vmem(K, C),
            vmem(GQ, 2 * C),
            vmem(2, 8, C),
            dma((14,)), dma((7,)),
            dma((SC,)), dma((SC,)),
            dma((MP,)), dma((MP,)),
            dma((MP,)), dma((MP,)),
            dma((SC,)), dma((SC,)),
            dma((MP,)), dma((MP,)),
            dma((SC,)), dma((SC,)),
        ],
        compiler_params=pltpu.CompilerParams(
            collective_id=0, has_side_effects=True, vmem_limit_bytes=VMEM_LIMIT
        ),
        name="exchange",
    )(
        base_rate.reshape(1, C),
        rate_moves,
        bond_block.reshape(1, B),
        bond_flows,
        group_id.reshape(1, M),
        issue_state.reshape(1, M),
        account_start.reshape(1, M),
        transition.transpose(1, 2, 0),
        benefit.reshape(1, S),
        guarantee.reshape(1, PG),
        spread.reshape(1, PG),
        lapse_base.reshape(1, PG),
        bond_target.reshape(B // C, C),
        start_rate,
    )
    occupancy, account_value, credited, value = pl.pallas_call(
        output_kernel,
        out_shape=[
            jax.ShapeDtypeStruct((S, C, M), F32),
            jax.ShapeDtypeStruct((C, M), F32),
            jax.ShapeDtypeStruct((16, C), F32),
            jax.ShapeDtypeStruct((1, 16), F32),
        ],
        in_specs=[in_hbm] * 7,
        out_specs=[in_hbm, in_hbm, in_vmem, in_vmem],
        scratch_shapes=[
            vmem(PG, 2 * C),
            vmem(2, PG, C),
            vmem(40, M),
            vmem(C, M),
            pltpu.VMEM((PG, M), BF16),
            vmem(32, C),
            vmem(SC, 8, C),
            vmem(S, C, M),
            vmem(C, M),
            dma((7,)),
            dma((2, C // CHUNK)),
        ],
        compiler_params=pltpu.CompilerParams(vmem_limit_bytes=VMEM_LIMIT),
        name="outputs",
    )(*between)
    return occupancy, account_value, credited.T, value.reshape(16)


def solution(mesh):
    placed = (
        P("mp"),
        P("mp"),
        P("mp"),
        P(),
        P(),
        P(),
        P("mp", None),
        P("mp", None),
        P("mp"),
        P("scen"),
        P(None, "scen"),
        P(),
        P(),
        P("scen", None),
    )
    return jax.shard_map(
        body,
        mesh=mesh,
        in_specs=placed,
        out_specs=(P(None, "scen", "mp"), P("scen", "mp"), P("scen", "mp"), P("mp")),
        check_vma=False,
    )
```

```python
import functools

import jax
import jax.numpy as jnp
from jax import lax
from jax.experimental import pallas as pl
from jax.experimental.pallas import tpu as pltpu
from jax.sharding import PartitionSpec as P

MESH = pl.DeviceIdType.MESH
EXACT = lax.Precision.HIGHEST
F32, BF16 = jnp.float32, jnp.bfloat16
STAY_WEIGHT = 40.0
LAPSE_SLOPE = 30.0
LIQUID_CHARGE = 0.5

S = 8
PG = 256
K = 256
DATES = 4
MONTHS = 3
C = 128
M = 1024
B = 2560
TILE = 256
MP = 16
SC = 16
SCEN = C * SC
KD = K // SC
GQ = 2 * PG // MP
VMEM_LIMIT = 56 * 1024 * 1024

NT = (((1,), (1,)), ((), ()))
NN = (((1,), (0,)), ((), ()))


def dot(a, b, dims, precision=None):
    return lax.dot_general(a, b, dims, precision=precision, preferred_element_type=F32)


def parts(x, count):
    found = []
    for _ in range(count):
        found.append(x.astype(BF16))
        x = x - found[-1].astype(F32)
    return found


def stack_parts(x, count, rows):
    found = parts(x, count)
    pieces = [piece.astype(F32) for piece in found]
    rest = rows - count * x.shape[0]
    if rest:
        pieces.append(jnp.zeros((rest, x.shape[1]), F32))
    return jnp.concatenate(pieces, axis=0).astype(BF16)


def iota(shape, axis):
    return lax.broadcasted_iota(jnp.int32, shape, axis)


def group_at(place):
    block = place // 16
    return (block // 4 * 4 + block % 2 * 2 + block // 2 % 2) * 16 + place % 16


def swap_blocks(rows):
    block = iota(rows.shape, 1) // 16 % 4
    width = rows.shape[1]
    up = pltpu.roll(rows, width - 16, 1)
    down = pltpu.roll(rows, 16, 1)
    return jnp.where(block == 1, up, jnp.where(block == 2, down, rows))


def discounts(rates, date):
    horizon = iota((K, C), 0)
    tenor = (horizon - date + 1).astype(F32) / 12.0
    factor = jnp.exp(-tenor * rates[date : date + 1, :])
    return jnp.where(horizon >= date, factor, 0.0) if date else factor


def exchange_kernel(
    base_hbm,
    moves_hbm,
    block_hbm,
    flows_hbm,
    group_hbm,
    state_hbm,
    account_hbm,
    transition_hbm,
    benefit_hbm,
    guarantee_hbm,
    spread_hbm,
    lapse_hbm,
    target_hbm,
    start_hbm,
    rho_hbm,
    pre_hbm,
    table_hbm,
    lapse1_hbm,
    point_hbm,
    small_hbm,
    value_hbm,
    pre_ref,
    table_ref,
    lapse1_ref,
    point_ref,
    small_ref,
    base_ref,
    moves_ref,
    block_ref,
    flows_ref,
    group_ref,
    state_ref,
    account_ref,
    transition_ref,
    benefit_ref,
    guarantee_ref,
    spread_ref,
    lapse_ref,
    target_ref,
    start_ref,
    flow_parts,
    chosen_ref,
    bond_ref,
    disc_ref,
    cols_ref,
    first_ref,
    a_src,
    a_buf,
    e_src,
    e_buf,
    b_src,
    b_buf,
    c_buf,
    d_src,
    f_src,
    load_sem,
    a_sems,
    b_sems,
    c_sems,
    d_first_sems,
    d_second_sems,
    e_sems,
    f_sems,
):
    d_sems = [d_first_sems, d_second_sems]
    mp, sc = lax.axis_index("mp"), lax.axis_index("scen")
    x, zh, core = mp // 4, mp // 2 % 2, mp % 2
    own = x * 2 + core
    zl, y = sc // 4, sc % 4

    def mp_index(dx, dz, dc):
        return (x + dx) % 4 * 4 + (zh + dz) % 2 * 2 + (core + dc) % 2

    def months_of(scen, half):
        return (scen // 4 + 2 * half) % 4 * 4 + scen % 4

    def scen_peer(dz, dy):
        there = (zl + dz) % 4
        across = (there - zl) * (there - zl) // 9
        return mp_index(0, across, 0), there * 4 + (y + dy) % 4

    steps = [(dz, dy) for dz in (2, 1, 3, 0) for dy in (2, 1, 3, 0) if (dz, dy) != (0, 0)]
    a_peers = [scen_peer(dz, dy) for dz, dy in steps]
    c_peers = [(mp, (zl + dz) % 4 * 4 + (y + dy) % 4) for dz, dy in steps]
    b_peers = [
        (mp_index(dx, dz, dc), (zl + 2 * dz) % 4 * 4 + y)
        for dz in (1, 0)
        for dx in (2, 1, 3, 0)
        for dc in (0, 1)
        if (dx, dz, dc) != (0, 0, 0)
    ]
    d_peers = [(mp_index(dx, 0, dc), sc) for dx in (2, 1, 3, 0) for dc in (0, 1) if (dx, dc) != (0, 0)]

    barrier = pltpu.get_barrier_semaphore()
    greeted = a_peers + b_peers + [peer for peer, (dz, dy) in zip(c_peers, steps) if dz in (1, 3)]
    for peer in greeted:
        pl.semaphore_signal(barrier, inc=1, device_id=peer, device_id_type=MESH)
    loads = [
        pltpu.make_async_copy(src, dst, load_sem.at[n])
        for n, (src, dst) in enumerate(
            [
                (base_hbm, base_ref),
                (moves_hbm, moves_ref),
                (block_hbm, block_ref),
                (flows_hbm, flows_ref),
                (group_hbm, group_ref),
                (state_hbm, state_ref),
                (account_hbm, account_ref),
                (transition_hbm, transition_ref),
                (benefit_hbm, benefit_ref),
                (guarantee_hbm, guarantee_ref),
                (spread_hbm, spread_ref),
                (lapse_hbm, lapse_ref),
                (target_hbm, target_ref),
                (start_hbm, start_ref),
            ]
        )
    ]
    for load in loads:
        load.start()

    def send_to(peers, src, dst, sems):
        for peer in peers:
            pltpu.make_async_remote_copy(
                src_ref=src(peer), dst_ref=dst, send_sem=sems.at[0], recv_sem=sems.at[1],
                device_id=peer, device_id_type=MESH,
            ).start()

    def all_of(peers, span, sems):
        return pltpu.make_async_remote_copy(
            src_ref=span, dst_ref=span, send_sem=sems.at[0], recv_sem=sems.at[1],
            device_id=peers[0], device_id_type=MESH,
        )

    def pair(peer):
        return peer[0] // 4 * 2 + peer[0] % 2

    a_all = all_of(a_peers, a_buf.at[: SC - 1], a_sems)
    b_all = all_of(b_peers, b_buf.at[: MP - 1], b_sems)
    c_all = all_of(c_peers, c_buf.at[: K - KD], c_sems)
    d_alls = [all_of(d_peers, rho_hbm.at[month, : PG - GQ], d_sems[month]) for month in range(MONTHS - 1)]
    e_all = all_of(b_peers, e_buf.at[: MP - 1], e_sems)
    f_all = all_of(a_peers, value_hbm.at[: SC - 1], f_sems)
    months = months_of(sc, zh)

    for load in loads[:2]:
        load.wait()
    rates = [base_ref[...]]
    for month in range(MONTHS):
        rates.append(rates[-1] + moves_ref[month : month + 1, :])
    rates = jnp.concatenate(rates, axis=0)
    blank = jnp.zeros((8, C), F32)
    small_ref[16:32, :] = jnp.concatenate([blank, rates, blank[:4]], axis=0)
    ones = jnp.ones((16, C), BF16)
    sums = []
    for date in range(DATES):
        pieces = parts(discounts(rates, date), 3)
        total = jnp.zeros((16, K), F32)
        for number, piece in enumerate(pieces):
            disc_ref[date, number] = piece
        for piece in reversed(pieces):
            total = total + dot(ones, piece, NT)
        sums.append(total[0:1])
    sums = jnp.concatenate(sums, axis=0)
    a_src[...] = jnp.concatenate([sums[:, : K // 2], sums[:, K // 2 :]], axis=0)

    pl.semaphore_wait(barrier, len(greeted))
    send_to(a_peers, lambda peer: a_src, a_buf.at[sc], a_sems)
    a_buf[sc] = a_src[...]

    for load in loads[2:4]:
        load.wait()
    picks = iota((32, K), 0)
    wanted = jnp.where(picks < KD, months * KD + picks, picks - KD)
    chosen = ((iota((32, K), 1) == wanted) & (picks < KD + MONTHS)).astype(BF16)
    bond_labels = group_at(iota((PG, TILE), 0))

    def prepare(tile, income):
        at = pl.ds(pl.multiple_of(tile * TILE, TILE), TILE)
        pieces = parts(flows_ref[at, :], 3)
        for number, piece in enumerate(pieces):
            flow_parts[number, at, :] = piece
        found = dot(chosen, pieces[2], NT) + dot(chosen, pieces[1], NT) + dot(chosen, pieces[0], NT)
        chosen_ref[:, at] = found[:KD]
        groups = (bond_labels == block_ref[:, at]).astype(BF16)
        bond_ref[:, at] = groups
        return income + dot(stack_parts(found[KD : KD + 8], 3, 32), groups, NT)

    income = lax.fori_loop(0, B // TILE, prepare, jnp.zeros((32, PG), F32))
    income = income[0:8] + income[8:16] + income[16:24]

    for load in loads[4:]:
        load.wait()
    accounts = jnp.zeros((32, PG), F32)
    for tile in range(M // TILE):
        at = pl.ds(tile * TILE, TILE)
        groups = (bond_labels == group_ref[:, at]).astype(BF16)
        point_ref[:, at] = groups
        mass = jnp.where(iota((S, TILE), 0) == state_ref[:, at], account_ref[:, at], 0.0)
        accounts = accounts + dot(stack_parts(mass, 3, 32), groups, NT)
    accounts = accounts[0:8] + accounts[8:16] + accounts[16:24]

    move = []
    for s in range(S):
        row = transition_ref[s] + jnp.where(iota((S, PG), 0) == s, STAY_WEIGHT, 0.0)
        move.append(row / jnp.sum(row, axis=0, keepdims=True))
    powers = [move]
    for _ in range(MONTHS - 1):
        last = powers[-1]
        powers.append([functools.reduce(jnp.add, [last[s][v : v + 1] * move[v] for v in range(S)]) for s in range(S)])
    benefit = jnp.where(iota((S, S), 0) == iota((S, S), 1), benefit_ref[...], 0.0)
    benefit = jnp.sum(benefit, axis=1, keepdims=True)
    stays = [jnp.concatenate([power[s][0:1] for s in range(S)], axis=0) for power in powers]
    pays = [
        jnp.concatenate([jnp.sum(power[s] * benefit, axis=0, keepdims=True) for s in range(S)], axis=0)
        for power in powers
    ]

    def by_state(rows):
        return jnp.sum(accounts * swap_blocks(rows), axis=0, keepdims=True)

    early = [accounts[0:1], by_state(stays[0]), by_state(stays[1]), by_state(pays[0]), by_state(pays[1]), by_state(pays[2])]
    early = jnp.concatenate(early + [jnp.zeros((2, PG), F32)], axis=0)
    for q in range(MP // 2):
        e_src[q] = jnp.concatenate(
            [early[:, q * GQ : (q + 1) * GQ], income[:, q * GQ : (q + 1) * GQ], jnp.zeros((8, C - 2 * GQ), F32)], axis=1
        )
    send_to(b_peers, lambda peer: e_src.at[pair(peer)], e_buf.at[mp], e_sems)
    e_buf[mp] = e_src[own]

    a_all.wait_recv()
    mean = a_buf[0]
    for slot in range(1, SC):
        mean = mean + a_buf[slot]
    mean = mean * (1.0 / SCEN)
    mean = stack_parts(jnp.concatenate([mean[0:4], mean[4:8]], axis=1), 3, 16)

    def weigh(tile, total):
        at = pl.ds(pl.multiple_of(tile * TILE, TILE), TILE)
        high = dot(mean, flow_parts[0, at, :], NT)
        middle = dot(mean, flow_parts[1, at, :], NT)
        low = dot(mean, flow_parts[2, at, :], NT)
        price = high[0:4] + ((high[4:8] + middle[0:4]) + (high[8:12] + middle[4:8] + low[0:4]))
        target = [target_ref[pl.ds(tile * 2 + n, 1), :] for n in range(2)]
        weight = jnp.concatenate(target, axis=1) / price
        flows = chosen_ref[:, at]
        scaled = jnp.concatenate([weight[date : date + 1] * flows for date in range(DATES)], axis=0)
        return total + dot(stack_parts(scaled, 3, 3 * DATES * KD), bond_ref[:, at], NT)

    worth = lax.fori_loop(0, B // TILE, weigh, jnp.zeros((3 * DATES * KD, PG), F32), unroll=True)
    size = DATES * KD
    worth = worth[0:size] + (worth[size : 2 * size] + worth[2 * size :])
    for q in range(MP // 2):
        b_src[q] = jnp.concatenate(
            [worth[date * KD : (date + 1) * KD, q * GQ : (q + 1) * GQ] for date in range(DATES)], axis=1
        )
    send_to(b_peers, lambda peer: b_src.at[pair(peer)], b_buf.at[mp], b_sems)
    b_buf[mp] = b_src[own]

    local = [guarantee_ref[...], spread_ref[...], lapse_ref[...], stays[0][0:1], stays[1][0:1], pays[0][0:1], pays[1][0:1], pays[2][0:1]]
    local = jnp.concatenate(local, axis=0)
    order = (group_at(iota((PG, PG), 0)) == iota((PG, PG), 1)).astype(F32)
    cols_ref[...] = dot(order, local, NT, EXACT)
    first_ref[...] = dot(order, start_ref[...], NT, EXACT)
    twice = jnp.broadcast_to(cols_ref[:, 2:3] * 2.0, (PG, C))
    pre_ref[0] = twice
    pre_ref[1] = first_ref[...]
    start_lapse = twice * jax.nn.sigmoid(LAPSE_SLOPE * (rates[0:1] - first_ref[...]))
    start_lapse = stack_parts(jnp.transpose(start_lapse), 2, 2 * C)

    gathered = jnp.concatenate(powers[2] + [powers[1][0], powers[0][0], stays[1], stays[0]], axis=0)
    gathered = stack_parts(swap_blocks(gathered), 2, 192)
    for tile in range(M // TILE):
        at = pl.ds(tile * TILE, TILE)
        found = dot(gathered, point_ref[:, at], NN)
        found = found[0:96] + found[96:192]
        states = state_ref[:, at]
        last = jnp.zeros((S, TILE), F32)
        for s in range(S):
            last = jnp.where(states == s, found[s * S : (s + 1) * S], last)
        held = iota((S, TILE), 0) == states
        second = jnp.sum(jnp.where(held, found[80:88], 0.0), axis=0, keepdims=True)
        first = jnp.sum(jnp.where(held, found[88:96], 0.0), axis=0, keepdims=True)
        start = (states == 0).astype(F32)
        lapsed = dot(start_lapse, point_ref[:, at], NN)
        lapse1_ref[:, at] = (lapsed[:C] + lapsed[C:]) * start
        table_ref[0:8, at] = last
        table_ref[8:16, at] = found[0:8]
        table_ref[16:24, at] = found[64:72]
        table_ref[24:32, at] = found[72:80]
        table_ref[32:40, at] = jnp.concatenate(
            [start, first, second, account_ref[:, at], jnp.zeros((4, TILE), F32)], axis=0
        )
    stores = [
        pltpu.make_async_copy(src, dst, load_sem.at[n])
        for n, (src, dst) in enumerate(
            [
                (pre_ref, pre_hbm),
                (table_ref, table_hbm),
                (lapse1_ref, lapse1_hbm),
                (point_ref, point_hbm),
            ]
        )
    ]
    for store in stores:
        store.start()

    b_all.wait_recv()
    total = b_buf[0]
    for slot in range(1, MP):
        total = total + b_buf[slot]
    rows = pl.ds(pl.multiple_of(months * KD, KD), KD)
    c_buf[rows, :] = total
    send_to(c_peers, lambda peer: c_buf.at[rows, :], c_buf.at[rows, :], c_sems)

    e_all.wait_recv()
    early = e_buf[0]
    for slot in range(1, MP):
        early = early + e_buf[slot]
    early = jnp.transpose(jnp.concatenate([early, jnp.zeros((C - 8, C), F32)], axis=0))
    income = early[GQ : 2 * GQ]
    mine = pl.ds(pl.multiple_of(own * GQ, GQ), GQ)
    columns = cols_ref[mine, :]
    guarantee, spread, lapse_base = columns[:, 0:1], columns[:, 1:2], columns[:, 2:3]
    stay = [columns[:, 3:4], columns[:, 4:5]]
    pay = [columns[:, 5:6], columns[:, 6:7], columns[:, 7:8]]
    credited = first_ref[mine, :]

    c_all.wait_recv()
    worth = jnp.transpose(c_buf[...])

    def assets_at(date):
        pieces = stack_parts(worth[date * GQ : (date + 1) * GQ], 3, 3 * GQ)
        high = dot(pieces, disc_ref[date, 0], NN)
        middle = dot(pieces[: 2 * GQ], disc_ref[date, 1], NN)
        low = dot(pieces[:GQ], disc_ref[date, 2], NN)
        return high[:GQ] + ((high[GQ : 2 * GQ] + middle[:GQ]) + (high[2 * GQ :] + middle[GQ:] + low))

    growth = jnp.ones((GQ, C), F32)
    present = jnp.zeros((GQ, C), F32)
    lapses = []
    held = assets_at(0)
    for month in range(MONTHS):
        factor = lapse_base * 2.0 * jax.nn.sigmoid(LAPSE_SLOPE * (rates[month : month + 1] - credited))
        mass = early[:GQ, month : month + 1]
        for lag, lapse in enumerate(reversed(lapses)):
            mass = mass - lapse * stay[lag]
        lapses.append(mass * factor)
        growth = growth * (1.0 + credited / 12.0)
        paid = early[:GQ, 3 + month : 4 + month]
        for lag, lapse in enumerate(reversed(lapses)):
            paid = paid - lapse * pay[lag]
        flows = growth * (lapses[-1] + paid)
        after = assets_at(month + 1)
        later = after + income[:, month : month + 1]
        earned = 12.0 * (later - held) / held
        credited = jnp.maximum(
            guarantee, 0.5 * credited + 0.5 * (earned - spread) - LIQUID_CHARGE * flows / held
        )
        if month < MONTHS - 1:
            d_src[month] = credited
            send_to(d_peers, lambda peer: d_src.at[month], rho_hbm.at[month, mine, :], d_sems[month])
        held = after
        present = present + flows * jnp.exp(-rates[month + 1 : month + 2] * ((month + 1) / 12.0))
    sums = dot(jnp.ones((8, C), F32), jnp.concatenate([present, jnp.zeros((C - GQ, C), F32)], axis=0), NT, EXACT)
    f_src[0] = sums
    f_src[1] = pltpu.roll(sums, C - 16, 1)
    send_to(a_peers, lambda peer: f_src.at[peer[0] // 2 % 2], value_hbm.at[sc], f_sems)
    small_ref[0:16, :] = 100.0 * jnp.where(zh == 0, credited[:16], credited[16:])
    late = [
        pltpu.make_async_copy(src, dst, load_sem.at[4 + n])
        for n, (src, dst) in enumerate(
            [
                (small_ref, small_hbm),
                (f_src.at[zh], value_hbm.at[sc]),
                (d_src.at[0], rho_hbm.at[0, mine, :]),
                (d_src.at[1], rho_hbm.at[1, mine, :]),
            ]
        )
    ]
    for store in late:
        store.start()
    for exchange in (a_all, e_all, b_all, c_all):
        exchange.wait_send()
    for store in stores + late:
        store.wait()
    for exchange in (*d_alls, f_all):
        exchange.wait_send()
        exchange.wait_recv()


CHUNK = 32


def output_kernel(
    rho_hbm, pre_hbm, table_hbm, lapse1_hbm, point_hbm, small_hbm, value_hbm,
    occupancy_hbm, account_hbm, credited_hbm, out_value_hbm,
    rho_ref, pre_ref, table_ref, lapse1_ref, point_ref, small_ref, sums_ref,
    occupancy_ref, account_ref, value_ref, load_sem, store_sem,
):
    loads = [
        pltpu.make_async_copy(src, dst, load_sem.at[n])
        for n, (src, dst) in enumerate(
            [
                (rho_hbm, rho_ref),
                (pre_hbm, pre_ref),
                (small_hbm, small_ref),
                (point_hbm, point_ref),
                (table_hbm, table_ref),
                (lapse1_hbm, lapse1_ref),
                (value_hbm, sums_ref),
            ]
        )
    ]
    for load in loads:
        load.start()
    for load in loads[:3]:
        load.wait()
    copies = [pltpu.make_async_copy(small_ref.at[0:16, :], credited_hbm, store_sem.at[0, C // CHUNK])]
    copies[0].start()
    twice = pre_ref[0]
    rho = [pre_ref[1], rho_ref[0], rho_ref[1]]
    tables = []
    for month in (1, 2):
        rates = small_ref[24 + month : 25 + month, :]
        tables.append(twice * jax.nn.sigmoid(LAPSE_SLOPE * (rates - rho[month])))
    grown = [rate * (1.0 / 12.0) for rate in rho]
    gain = grown[0] + grown[1] + grown[0] * grown[1]
    tables.append(gain + grown[2] + gain * grown[2])
    tables = [parts(jnp.transpose(table), 2) for table in tables]

    for load in loads[3:]:
        load.wait()
    value = sums_ref[0]
    for slot in range(1, SC):
        value = value + sums_ref[slot]
    value_ref[...] = value[0:1, 0:16] * (1.0 / SCEN)
    copies.append(pltpu.make_async_copy(value_ref, out_value_hbm, store_sem.at[1, C // CHUNK]))
    copies[-1].start()
    for chunk in range(C // CHUNK):
        rows = slice(chunk * CHUNK, (chunk + 1) * CHUNK)
        lhs = jnp.concatenate([piece[rows] for table in tables for piece in table], axis=0)
        for tile in range(M // TILE):
            at = pl.ds(tile * TILE, TILE)
            found = dot(lhs, point_ref[:, at], NN)
            found = [
                found[2 * n * CHUNK : (2 * n + 1) * CHUNK] + found[(2 * n + 1) * CHUNK : (2 * n + 2) * CHUNK]
                for n in range(3)
            ]
            first = lapse1_ref[rows, at]
            second = (table_ref[33:34, at] - first * table_ref[24:25, at]) * found[0]
            third = (table_ref[34:35, at] - first * table_ref[16:17, at] - second * table_ref[24:25, at]) * found[1]
            for u in range(S):
                occupancy_ref[u, rows, at] = (
                    table_ref[u : u + 1, at]
                    - first * table_ref[8 + u : 9 + u, at]
                    - second * table_ref[16 + u : 17 + u, at]
                    - third * table_ref[24 + u : 25 + u, at]
                )
            account = table_ref[35:36, at]
            account_ref[rows, at] = account + account * found[2]
        copies.append(
            pltpu.make_async_copy(occupancy_ref.at[:, rows, :], occupancy_hbm.at[:, rows, :], store_sem.at[0, chunk])
        )
        copies.append(pltpu.make_async_copy(account_ref.at[rows, :], account_hbm.at[rows, :], store_sem.at[1, chunk]))
        copies[-2].start()
        copies[-1].start()
    for copy in copies:
        copy.wait()


def vmem(*shape):
    return pltpu.VMEM(shape, F32)


def body(
    group_id,
    issue_state,
    account_start,
    transition,
    lapse_base,
    benefit,
    bond_block,
    bond_flows,
    bond_target,
    base_rate,
    rate_moves,
    guarantee,
    spread,
    start_rate,
):
    in_hbm = pl.BlockSpec(memory_space=pltpu.HBM)
    dma = pltpu.SemaphoreType.DMA
    between = pl.pallas_call(
        exchange_kernel,
        out_shape=[
            jax.ShapeDtypeStruct((2, PG, C), F32),
            jax.ShapeDtypeStruct((2, PG, C), F32),
            jax.ShapeDtypeStruct((40, M), F32),
            jax.ShapeDtypeStruct((C, M), F32),
            jax.ShapeDtypeStruct((PG, M), BF16),
            jax.ShapeDtypeStruct((32, C), F32),
            jax.ShapeDtypeStruct((SC, 8, C), F32),
        ],
        in_specs=[in_hbm] * 14,
        out_specs=[in_hbm] * 7,
        scratch_shapes=[
            vmem(2, PG, C),
            vmem(40, M),
            vmem(C, M),
            pltpu.VMEM((PG, M), BF16),
            vmem(32, C),
            vmem(1, C),
            vmem(MONTHS, C),
            pltpu.VMEM((1, B), jnp.int32),
            vmem(B, K),
            pltpu.VMEM((1, M), jnp.int32),
            pltpu.VMEM((1, M), jnp.int32),
            vmem(1, M),
            vmem(S, S, PG),
            vmem(1, S),
            vmem(1, PG),
            vmem(1, PG),
            vmem(1, PG),
            vmem(B // C, C),
            vmem(C, PG),
            pltpu.VMEM((3, B, K), BF16),
            vmem(KD, B),
            pltpu.VMEM((PG, B), BF16),
            pltpu.VMEM((DATES, 3, K, C), BF16),
            vmem(PG, 8),
            vmem(PG, C),
            vmem(8, C),
            vmem(SC, 8, C),
            vmem(MP // 2, 8, C),
            vmem(MP, 8, C),
            vmem(MP // 2, KD, C),
            vmem(MP, KD, C),
            vmem(K, C),
            vmem(2, GQ, C),
            vmem(2, 8, C),
            dma((14,)),
            *[dma((2,)) for _ in range(7)],
        ],
        compiler_params=pltpu.CompilerParams(
            collective_id=0, has_side_effects=True, vmem_limit_bytes=VMEM_LIMIT
        ),
        name="exchange",
    )(
        base_rate.reshape(1, C),
        rate_moves,
        bond_block.reshape(1, B),
        bond_flows,
        group_id.reshape(1, M),
        issue_state.reshape(1, M),
        account_start.reshape(1, M),
        transition.transpose(1, 2, 0),
        benefit.reshape(1, S),
        guarantee.reshape(1, PG),
        spread.reshape(1, PG),
        lapse_base.reshape(1, PG),
        bond_target.reshape(B // C, C),
        start_rate,
    )
    occupancy, account_value, credited, value = pl.pallas_call(
        output_kernel,
        out_shape=[
            jax.ShapeDtypeStruct((S, C, M), F32),
            jax.ShapeDtypeStruct((C, M), F32),
            jax.ShapeDtypeStruct((16, C), F32),
            jax.ShapeDtypeStruct((1, 16), F32),
        ],
        in_specs=[in_hbm] * 7,
        out_specs=[in_hbm] * 4,
        scratch_shapes=[
            vmem(2, PG, C),
            vmem(2, PG, C),
            vmem(40, M),
            vmem(C, M),
            pltpu.VMEM((PG, M), BF16),
            vmem(32, C),
            vmem(SC, 8, C),
            vmem(S, C, M),
            vmem(C, M),
            vmem(1, 16),
            dma((7,)),
            dma((2, C // CHUNK + 1)),
        ],
        compiler_params=pltpu.CompilerParams(vmem_limit_bytes=VMEM_LIMIT),
        name="outputs",
    )(*between)
    return occupancy, account_value, credited.T, value.reshape(16)


def solution(mesh):
    placed = (
        P("mp"),
        P("mp"),
        P("mp"),
        P(),
        P(),
        P(),
        P("mp", None),
        P("mp", None),
        P("mp"),
        P("scen"),
        P(None, "scen"),
        P(),
        P(),
        P("scen", None),
    )
    return jax.shard_map(
        body,
        mesh=mesh,
        in_specs=placed,
        out_specs=(P(None, "scen", "mp"), P("scen", "mp"), P("scen", "mp"), P("mp")),
        check_vma=False,
    )
```

```python
import functools

import jax
import jax.numpy as jnp
from jax import lax
from jax.experimental import pallas as pl
from jax.experimental.pallas import tpu as pltpu
from jax.sharding import PartitionSpec as P

MESH = pl.DeviceIdType.MESH
EXACT = lax.Precision.HIGHEST
F32, BF16 = jnp.float32, jnp.bfloat16
STAY_WEIGHT = 40.0
LAPSE_SLOPE = 30.0
LIQUID_CHARGE = 0.5

S = 8
PG = 256
K = 256
DATES = 4
MONTHS = 3
C = 128
M = 1024
B = 2560
TILE = 256
MP = 16
SC = 16
SCEN = C * SC
KD = K // SC
GQ = 2 * PG // MP
VMEM_LIMIT = 56 * 1024 * 1024

NT = (((1,), (1,)), ((), ()))
NN = (((1,), (0,)), ((), ()))


def dot(a, b, dims, precision=None):
    return lax.dot_general(a, b, dims, precision=precision, preferred_element_type=F32)


def parts(x, count):
    found = []
    for _ in range(count):
        found.append(x.astype(BF16))
        x = x - found[-1].astype(F32)
    return found


def stack_parts(x, count, rows):
    found = parts(x, count)
    pieces = [piece.astype(F32) for piece in found]
    rest = rows - count * x.shape[0]
    if rest:
        pieces.append(jnp.zeros((rest, x.shape[1]), F32))
    return jnp.concatenate(pieces, axis=0).astype(BF16)


def iota(shape, axis):
    return lax.broadcasted_iota(jnp.int32, shape, axis)


def group_at(place):
    block = place // 16
    return (block // 4 * 4 + block % 2 * 2 + block // 2 % 2) * 16 + place % 16


def swap_blocks(rows):
    block = iota(rows.shape, 1) // 16 % 4
    width = rows.shape[1]
    up = pltpu.roll(rows, width - 16, 1)
    down = pltpu.roll(rows, 16, 1)
    return jnp.where(block == 1, up, jnp.where(block == 2, down, rows))


def discounts(rates, date):
    horizon = iota((K, C), 0)
    tenor = (horizon - date + 1).astype(F32) / 12.0
    factor = jnp.exp(-tenor * rates[date : date + 1, :])
    return jnp.where(horizon >= date, factor, 0.0) if date else factor


def exchange_kernel(
    base_hbm,
    moves_hbm,
    block_hbm,
    flows_hbm,
    group_hbm,
    state_hbm,
    account_hbm,
    transition_hbm,
    benefit_hbm,
    guarantee_hbm,
    spread_hbm,
    lapse_hbm,
    target_hbm,
    start_hbm,
    rho_hbm,
    pre_hbm,
    table_hbm,
    lapse1_hbm,
    small_hbm,
    value_hbm,
    pre_ref,
    table_ref,
    lapse1_ref,
    small_ref,
    base_ref,
    moves_ref,
    block_ref,
    flows_ref,
    group_ref,
    state_ref,
    account_ref,
    transition_ref,
    benefit_ref,
    guarantee_ref,
    spread_ref,
    lapse_ref,
    target_ref,
    start_ref,
    flow_parts,
    chosen_ref,
    bond_ref,
    point_ref,
    disc_ref,
    cols_ref,
    first_ref,
    a_src,
    a_buf,
    e_src,
    e_buf,
    b_src,
    b_buf,
    c_buf,
    d_src,
    f_src,
    load_sem,
    a_sems,
    b_sems,
    c_sems,
    d_first_sems,
    d_second_sems,
    e_sems,
    f_sems,
):
    d_sems = [d_first_sems, d_second_sems]
    mp, sc = lax.axis_index("mp"), lax.axis_index("scen")
    x, zh, core = mp // 4, mp // 2 % 2, mp % 2
    own = x * 2 + core
    zl, y = sc // 4, sc % 4

    def mp_index(dx, dz, dc):
        return (x + dx) % 4 * 4 + (zh + dz) % 2 * 2 + (core + dc) % 2

    def months_of(scen, half):
        return (scen // 4 + 2 * half) % 4 * 4 + scen % 4

    def scen_peer(dz, dy):
        there = (zl + dz) % 4
        across = (there - zl) * (there - zl) // 9
        return mp_index(0, across, 0), there * 4 + (y + dy) % 4

    steps = [(dz, dy) for dz in (2, 1, 3, 0) for dy in (2, 1, 3, 0) if (dz, dy) != (0, 0)]
    a_peers = [scen_peer(dz, dy) for dz, dy in steps]
    c_peers = [(mp, (zl + dz) % 4 * 4 + (y + dy) % 4) for dz, dy in steps]
    b_peers = [
        (mp_index(dx, dz, dc), (zl + 2 * dz) % 4 * 4 + y)
        for dz in (1, 0)
        for dx in (2, 1, 3, 0)
        for dc in (0, 1)
        if (dx, dz, dc) != (0, 0, 0)
    ]
    d_peers = [(mp_index(dx, 0, dc), sc) for dx in (2, 1, 3, 0) for dc in (0, 1) if (dx, dc) != (0, 0)]

    barrier = pltpu.get_barrier_semaphore()
    greeted = a_peers + b_peers
    for peer in greeted:
        pl.semaphore_signal(barrier, inc=1, device_id=peer, device_id_type=MESH)
    loads = [
        pltpu.make_async_copy(src, dst, load_sem.at[n])
        for n, (src, dst) in enumerate(
            [
                (base_hbm, base_ref),
                (moves_hbm, moves_ref),
                (block_hbm, block_ref),
                (flows_hbm, flows_ref),
                (group_hbm, group_ref),
                (state_hbm, state_ref),
                (account_hbm, account_ref),
                (transition_hbm, transition_ref),
                (benefit_hbm, benefit_ref),
                (guarantee_hbm, guarantee_ref),
                (spread_hbm, spread_ref),
                (lapse_hbm, lapse_ref),
                (target_hbm, target_ref),
                (start_hbm, start_ref),
            ]
        )
    ]
    for load in loads:
        load.start()

    def send_to(peers, src, dst, sems):
        for peer in peers:
            pltpu.make_async_remote_copy(
                src_ref=src(peer), dst_ref=dst, send_sem=sems.at[0], recv_sem=sems.at[1],
                device_id=peer, device_id_type=MESH,
            ).start()

    def all_of(peers, span, sems):
        return pltpu.make_async_remote_copy(
            src_ref=span, dst_ref=span, send_sem=sems.at[0], recv_sem=sems.at[1],
            device_id=peers[0], device_id_type=MESH,
        )

    def pair(peer):
        return peer[0] // 4 * 2 + peer[0] % 2

    a_all = all_of(a_peers, a_buf.at[: SC - 1], a_sems)
    b_all = all_of(b_peers, b_buf.at[: MP - 1], b_sems)
    c_all = all_of(c_peers, c_buf.at[: K - KD], c_sems)
    d_alls = [all_of(d_peers, rho_hbm.at[month, : PG - GQ], d_sems[month]) for month in range(MONTHS - 1)]
    e_all = all_of(b_peers, e_buf.at[: MP - 1], e_sems)
    f_all = all_of(a_peers, value_hbm.at[: SC - 1], f_sems)
    months = months_of(sc, zh)

    for load in loads[:2]:
        load.wait()
    rates = [base_ref[...]]
    for month in range(MONTHS):
        rates.append(rates[-1] + moves_ref[month : month + 1, :])
    rates = jnp.concatenate(rates, axis=0)
    blank = jnp.zeros((8, C), F32)
    small_ref[16:32, :] = jnp.concatenate([blank, rates, blank[:4]], axis=0)
    ones = jnp.ones((16, C), BF16)
    sums = []
    for date in range(DATES):
        pieces = parts(discounts(rates, date), 3)
        total = jnp.zeros((16, K), F32)
        for number, piece in enumerate(pieces):
            disc_ref[date, number] = piece
        for piece in reversed(pieces):
            total = total + dot(ones, piece, NT)
        sums.append(total[0:1])
    sums = jnp.concatenate(sums, axis=0)
    a_src[...] = jnp.concatenate([sums[:, : K // 2], sums[:, K // 2 :]], axis=0)

    pl.semaphore_wait(barrier, len(greeted))
    send_to(a_peers, lambda peer: a_src, a_buf.at[sc], a_sems)
    a_buf[sc] = a_src[...]

    for load in loads[2:4]:
        load.wait()
    picks = iota((32, K), 0)
    wanted = jnp.where(picks < KD, months * KD + picks, picks - KD)
    chosen = ((iota((32, K), 1) == wanted) & (picks < KD + MONTHS)).astype(BF16)
    bond_labels = group_at(iota((PG, TILE), 0))

    def prepare(tile, income):
        at = pl.ds(pl.multiple_of(tile * TILE, TILE), TILE)
        pieces = parts(flows_ref[at, :], 3)
        for number in range(2):
            flow_parts[number, at, :] = pieces[number]
        found = dot(chosen, pieces[2], NT) + dot(chosen, pieces[1], NT) + dot(chosen, pieces[0], NT)
        chosen_ref[:, at] = found[:KD]
        groups = (bond_labels == block_ref[:, at]).astype(BF16)
        bond_ref[:, at] = groups
        return income + dot(stack_parts(found[KD : KD + 8], 3, 32), groups, NT)

    income = lax.fori_loop(0, B // TILE, prepare, jnp.zeros((32, PG), F32), unroll=2)
    income = income[0:8] + income[8:16] + income[16:24]

    for load in loads[4:]:
        load.wait()
    accounts = jnp.zeros((32, PG), F32)
    for tile in range(M // TILE):
        at = pl.ds(tile * TILE, TILE)
        groups = (bond_labels == group_ref[:, at]).astype(BF16)
        point_ref[:, at] = groups
        mass = jnp.where(iota((S, TILE), 0) == state_ref[:, at], account_ref[:, at], 0.0)
        accounts = accounts + dot(stack_parts(mass, 3, 32), groups, NT)
    accounts = accounts[0:8] + accounts[8:16] + accounts[16:24]

    move = []
    for s in range(S):
        row = transition_ref[s] + jnp.where(iota((S, PG), 0) == s, STAY_WEIGHT, 0.0)
        move.append(row / jnp.sum(row, axis=0, keepdims=True))
    powers = [move]
    for _ in range(MONTHS - 1):
        last = powers[-1]
        powers.append([functools.reduce(jnp.add, [last[s][v : v + 1] * move[v] for v in range(S)]) for s in range(S)])
    benefit = jnp.where(iota((S, S), 0) == iota((S, S), 1), benefit_ref[...], 0.0)
    benefit = jnp.sum(benefit, axis=1, keepdims=True)
    stays = [jnp.concatenate([power[s][0:1] for s in range(S)], axis=0) for power in powers]
    pays = [
        jnp.concatenate([jnp.sum(power[s] * benefit, axis=0, keepdims=True) for s in range(S)], axis=0)
        for power in powers
    ]

    def by_state(rows):
        return jnp.sum(accounts * swap_blocks(rows), axis=0, keepdims=True)

    early = [accounts[0:1], by_state(stays[0]), by_state(stays[1]), by_state(pays[0]), by_state(pays[1]), by_state(pays[2])]
    early = jnp.concatenate(early + [jnp.zeros((2, PG), F32)], axis=0)
    for q in range(MP // 2):
        e_src[q] = jnp.concatenate(
            [early[:, q * GQ : (q + 1) * GQ], income[:, q * GQ : (q + 1) * GQ], jnp.zeros((8, C - 2 * GQ), F32)], axis=1
        )
    send_to(b_peers, lambda peer: e_src.at[pair(peer)], e_buf.at[mp], e_sems)
    e_buf[mp] = e_src[own]

    a_all.wait_recv()
    mean = a_buf[0]
    for slot in range(1, SC):
        mean = mean + a_buf[slot]
    mean = mean * (1.0 / SCEN)
    mean = stack_parts(jnp.concatenate([mean[0:4], mean[4:8]], axis=1), 3, 16)

    def weigh(tile, total):
        at = pl.ds(pl.multiple_of(tile * TILE, TILE), TILE)
        high = dot(mean, flow_parts[0, at, :], NT)
        middle = dot(mean, flow_parts[1, at, :], NT)
        price = high[0:4] + ((high[4:8] + middle[0:4]) + (high[8:12] + middle[4:8]))
        target = [target_ref[pl.ds(tile * 2 + n, 1), :] for n in range(2)]
        weight = jnp.concatenate(target, axis=1) / price
        flows = chosen_ref[:, at]
        scaled = jnp.concatenate([weight[date : date + 1] * flows for date in range(DATES)], axis=0)
        return total + dot(stack_parts(scaled, 3, 3 * DATES * KD), bond_ref[:, at], NT)

    worth = lax.fori_loop(0, B // TILE, weigh, jnp.zeros((3 * DATES * KD, PG), F32), unroll=True)
    size = DATES * KD
    worth = worth[0:size] + (worth[size : 2 * size] + worth[2 * size :])
    for q in range(MP // 2):
        b_src[q] = jnp.concatenate(
            [worth[date * KD : (date + 1) * KD, q * GQ : (q + 1) * GQ] for date in range(DATES)], axis=1
        )
    send_to(b_peers, lambda peer: b_src.at[pair(peer)], b_buf.at[mp], b_sems)
    b_buf[mp] = b_src[own]

    local = [guarantee_ref[...], spread_ref[...], lapse_ref[...], stays[0][0:1], stays[1][0:1], pays[0][0:1], pays[1][0:1], pays[2][0:1]]
    local = jnp.concatenate(local, axis=0)
    order = (group_at(iota((PG, PG), 0)) == iota((PG, PG), 1)).astype(F32)
    cols_ref[...] = dot(order, local, NT, EXACT)
    first_ref[...] = dot(order, start_ref[...], NT, EXACT)
    twice = jnp.broadcast_to(cols_ref[:, 2:3] * 2.0, (PG, C))
    pre_ref[0] = twice
    pre_ref[1] = first_ref[...]
    start_lapse = twice * jax.nn.sigmoid(LAPSE_SLOPE * (rates[0:1] - first_ref[...]))
    start_lapse = stack_parts(jnp.transpose(start_lapse), 2, 2 * C)

    gathered = jnp.concatenate(powers[2] + [powers[1][0], powers[0][0], stays[1], stays[0]], axis=0)
    gathered = stack_parts(swap_blocks(gathered), 2, 192)
    for tile in range(M // TILE):
        at = pl.ds(tile * TILE, TILE)
        found = dot(gathered, point_ref[:, at], NN)
        found = found[0:96] + found[96:192]
        states = state_ref[:, at]
        last = jnp.zeros((S, TILE), F32)
        for s in range(S):
            last = jnp.where(states == s, found[s * S : (s + 1) * S], last)
        held = iota((S, TILE), 0) == states
        second = jnp.sum(jnp.where(held, found[80:88], 0.0), axis=0, keepdims=True)
        first = jnp.sum(jnp.where(held, found[88:96], 0.0), axis=0, keepdims=True)
        start = (states == 0).astype(F32)
        lapsed = dot(start_lapse, point_ref[:, at], NN)
        lapse1_ref[:, at] = (lapsed[:C] + lapsed[C:]) * start
        table_ref[0:8, at] = last
        table_ref[8:16, at] = found[0:8]
        table_ref[16:24, at] = found[64:72]
        table_ref[24:32, at] = found[72:80]
        table_ref[32:40, at] = jnp.concatenate(
            [start, first, second, account_ref[:, at], group_ref[:, at].astype(F32), jnp.zeros((3, TILE), F32)],
            axis=0,
        )
    stores = [
        pltpu.make_async_copy(src, dst, load_sem.at[n])
        for n, (src, dst) in enumerate(
            [
                (pre_ref, pre_hbm),
                (table_ref, table_hbm),
                (lapse1_ref, lapse1_hbm),
            ]
        )
    ]
    for store in stores:
        store.start()

    b_all.wait_recv()
    total = b_buf[0]
    for slot in range(1, MP):
        total = total + b_buf[slot]
    rows = pl.ds(pl.multiple_of(months * KD, KD), KD)
    c_buf[rows, :] = total
    send_to(c_peers, lambda peer: c_buf.at[rows, :], c_buf.at[rows, :], c_sems)

    e_all.wait_recv()
    early = e_buf[0]
    for slot in range(1, MP):
        early = early + e_buf[slot]
    early = jnp.transpose(jnp.concatenate([early, jnp.zeros((C - 8, C), F32)], axis=0))
    income = early[GQ : 2 * GQ]
    mine = pl.ds(pl.multiple_of(own * GQ, GQ), GQ)
    columns = cols_ref[mine, :]
    guarantee, spread, lapse_base = columns[:, 0:1], columns[:, 1:2], columns[:, 2:3]
    stay = [columns[:, 3:4], columns[:, 4:5]]
    pay = [columns[:, 5:6], columns[:, 6:7], columns[:, 7:8]]
    credited = first_ref[mine, :]

    c_all.wait_recv()
    worth = jnp.transpose(c_buf[...])

    def assets_at(date):
        pieces = stack_parts(worth[date * GQ : (date + 1) * GQ], 3, 3 * GQ)
        high = dot(pieces, disc_ref[date, 0], NN)
        middle = dot(pieces[: 2 * GQ], disc_ref[date, 1], NN)
        low = dot(pieces[:GQ], disc_ref[date, 2], NN)
        return high[:GQ] + ((high[GQ : 2 * GQ] + middle[:GQ]) + (high[2 * GQ :] + middle[GQ:] + low))

    growth = jnp.ones((GQ, C), F32)
    present = jnp.zeros((GQ, C), F32)
    lapses = []
    held = assets_at(0)
    for month in range(MONTHS):
        factor = lapse_base * 2.0 * jax.nn.sigmoid(LAPSE_SLOPE * (rates[month : month + 1] - credited))
        mass = early[:GQ, month : month + 1]
        for lag, lapse in enumerate(reversed(lapses)):
            mass = mass - lapse * stay[lag]
        lapses.append(mass * factor)
        growth = growth * (1.0 + credited / 12.0)
        paid = early[:GQ, 3 + month : 4 + month]
        for lag, lapse in enumerate(reversed(lapses)):
            paid = paid - lapse * pay[lag]
        flows = growth * (lapses[-1] + paid)
        after = assets_at(month + 1)
        later = after + income[:, month : month + 1]
        earned = 12.0 * (later - held) / held
        credited = jnp.maximum(
            guarantee, 0.5 * credited + 0.5 * (earned - spread) - LIQUID_CHARGE * flows / held
        )
        if month < MONTHS - 1:
            d_src[month] = credited
            send_to(d_peers, lambda peer: d_src.at[month], rho_hbm.at[month, mine, :], d_sems[month])
        held = after
        present = present + flows * jnp.exp(-rates[month + 1 : month + 2] * ((month + 1) / 12.0))
    sums = dot(jnp.ones((8, C), F32), jnp.concatenate([present, jnp.zeros((C - GQ, C), F32)], axis=0), NT, EXACT)
    f_src[0] = sums
    f_src[1] = pltpu.roll(sums, C - 16, 1)
    send_to(a_peers, lambda peer: f_src.at[peer[0] // 2 % 2], value_hbm.at[sc], f_sems)
    small_ref[0:16, :] = 100.0 * jnp.where(zh == 0, credited[:16], credited[16:])
    late = [
        pltpu.make_async_copy(src, dst, load_sem.at[4 + n])
        for n, (src, dst) in enumerate(
            [
                (small_ref, small_hbm),
                (f_src.at[zh], value_hbm.at[sc]),
                (d_src.at[0], rho_hbm.at[0, mine, :]),
                (d_src.at[1], rho_hbm.at[1, mine, :]),
            ]
        )
    ]
    for store in late:
        store.start()
    for exchange in (a_all, e_all, b_all, c_all):
        exchange.wait_send()
    for store in stores + late:
        store.wait()
    for exchange in (*d_alls, f_all):
        exchange.wait_send()
        exchange.wait_recv()


CHUNK = 16


def output_kernel(
    rho_hbm, pre_hbm, table_hbm, lapse1_hbm, small_hbm, value_hbm,
    occupancy_hbm, account_hbm, credited_hbm, out_value_hbm,
    rho_ref, pre_ref, table_ref, lapse1_ref, point_ref, small_ref, sums_ref,
    occupancy_ref, account_ref, value_ref, load_sem, store_sem,
):
    loads = [
        pltpu.make_async_copy(src, dst, load_sem.at[n])
        for n, (src, dst) in enumerate(
            [
                (rho_hbm, rho_ref),
                (pre_hbm, pre_ref),
                (small_hbm, small_ref),
                (table_hbm, table_ref),
                (lapse1_hbm.at[:CHUNK], lapse1_ref.at[:CHUNK]),
                (lapse1_hbm.at[CHUNK:], lapse1_ref.at[CHUNK:]),
                (value_hbm, sums_ref),
            ]
        )
    ]
    for load in loads:
        load.start()
    for load in loads[:3]:
        load.wait()
    copies = [pltpu.make_async_copy(small_ref.at[0:16, :], credited_hbm, store_sem.at[2])]
    copies[0].start()
    twice = pre_ref[0]
    rho = [pre_ref[1], rho_ref[0], rho_ref[1]]
    tables = []
    for month in (1, 2):
        rates = small_ref[24 + month : 25 + month, :]
        tables.append(twice * jax.nn.sigmoid(LAPSE_SLOPE * (rates - rho[month])))
    grown = [rate * (1.0 / 12.0) for rate in rho]
    gain = grown[0] + grown[1] + grown[0] * grown[1]
    tables.append(gain + grown[2] + gain * grown[2])
    tables = [parts(jnp.transpose(table), 2) for table in tables]

    loads[3].wait()
    labels = group_at(iota((PG, TILE), 0)).astype(F32)
    for tile in range(M // TILE):
        at = pl.ds(tile * TILE, TILE)
        point_ref[:, at] = (labels == table_ref[36:37, at]).astype(BF16)
    loads[4].wait()
    for chunk in range(C // CHUNK):
        rows = slice(chunk * CHUNK, (chunk + 1) * CHUNK)
        lhs = jnp.concatenate([piece[rows] for table in tables for piece in table], axis=0)
        for tile in range(M // TILE):
            at = pl.ds(tile * TILE, TILE)
            found = dot(lhs, point_ref[:, at], NN)
            found = [
                found[2 * n * CHUNK : (2 * n + 1) * CHUNK] + found[(2 * n + 1) * CHUNK : (2 * n + 2) * CHUNK]
                for n in range(3)
            ]
            first = lapse1_ref[rows, at]
            second = (table_ref[33:34, at] - first * table_ref[24:25, at]) * found[0]
            third = (table_ref[34:35, at] - first * table_ref[16:17, at] - second * table_ref[24:25, at]) * found[1]
            for u in range(S):
                occupancy_ref[u, rows, at] = (
                    table_ref[u : u + 1, at]
                    - first * table_ref[8 + u : 9 + u, at]
                    - second * table_ref[16 + u : 17 + u, at]
                    - third * table_ref[24 + u : 25 + u, at]
                )
            account = table_ref[35:36, at]
            account_ref[rows, at] = account + account * found[2]
        pltpu.make_async_copy(occupancy_ref.at[:, rows, :], occupancy_hbm.at[:, rows, :], store_sem.at[0]).start()
        pltpu.make_async_copy(account_ref.at[rows, :], account_hbm.at[rows, :], store_sem.at[1]).start()
        if chunk == 0:
            for load in loads[5:]:
                load.wait()
            value = sums_ref[0]
            for slot in range(1, SC):
                value = value + sums_ref[slot]
            value_ref[...] = value[0:1, 0:16] * (1.0 / SCEN)
            copies.append(pltpu.make_async_copy(value_ref, out_value_hbm, store_sem.at[3]))
            copies[-1].start()
    copies.append(pltpu.make_async_copy(occupancy_ref, occupancy_hbm, store_sem.at[0]))
    copies.append(pltpu.make_async_copy(account_ref, account_hbm, store_sem.at[1]))
    for copy in copies:
        copy.wait()


def vmem(*shape):
    return pltpu.VMEM(shape, F32)


def body(
    group_id,
    issue_state,
    account_start,
    transition,
    lapse_base,
    benefit,
    bond_block,
    bond_flows,
    bond_target,
    base_rate,
    rate_moves,
    guarantee,
    spread,
    start_rate,
):
    in_hbm = pl.BlockSpec(memory_space=pltpu.HBM)
    dma = pltpu.SemaphoreType.DMA
    between = pl.pallas_call(
        exchange_kernel,
        out_shape=[
            jax.ShapeDtypeStruct((2, PG, C), F32),
            jax.ShapeDtypeStruct((2, PG, C), F32),
            jax.ShapeDtypeStruct((40, M), F32),
            jax.ShapeDtypeStruct((C, M), F32),
            jax.ShapeDtypeStruct((32, C), F32),
            jax.ShapeDtypeStruct((SC, 8, C), F32),
        ],
        in_specs=[in_hbm] * 14,
        out_specs=[in_hbm] * 6,
        scratch_shapes=[
            vmem(2, PG, C),
            vmem(40, M),
            vmem(C, M),
            vmem(32, C),
            vmem(1, C),
            vmem(MONTHS, C),
            pltpu.VMEM((1, B), jnp.int32),
            vmem(B, K),
            pltpu.VMEM((1, M), jnp.int32),
            pltpu.VMEM((1, M), jnp.int32),
            vmem(1, M),
            vmem(S, S, PG),
            vmem(1, S),
            vmem(1, PG),
            vmem(1, PG),
            vmem(1, PG),
            vmem(B // C, C),
            vmem(C, PG),
            pltpu.VMEM((2, B, K), BF16),
            vmem(KD, B),
            pltpu.VMEM((PG, B), BF16),
            pltpu.VMEM((PG, M), BF16),
            pltpu.VMEM((DATES, 3, K, C), BF16),
            vmem(PG, 8),
            vmem(PG, C),
            vmem(8, C),
            vmem(SC, 8, C),
            vmem(MP // 2, 8, C),
            vmem(MP, 8, C),
            vmem(MP // 2, KD, C),
            vmem(MP, KD, C),
            vmem(K, C),
            vmem(2, GQ, C),
            vmem(2, 8, C),
            dma((14,)),
            *[dma((2,)) for _ in range(7)],
        ],
        compiler_params=pltpu.CompilerParams(
            collective_id=0, has_side_effects=True, vmem_limit_bytes=VMEM_LIMIT
        ),
        name="exchange",
    )(
        base_rate.reshape(1, C),
        rate_moves,
        bond_block.reshape(1, B),
        bond_flows,
        group_id.reshape(1, M),
        issue_state.reshape(1, M),
        account_start.reshape(1, M),
        transition.transpose(1, 2, 0),
        benefit.reshape(1, S),
        guarantee.reshape(1, PG),
        spread.reshape(1, PG),
        lapse_base.reshape(1, PG),
        bond_target.reshape(B // C, C),
        start_rate,
    )
    occupancy, account_value, credited, value = pl.pallas_call(
        output_kernel,
        out_shape=[
            jax.ShapeDtypeStruct((S, C, M), F32),
            jax.ShapeDtypeStruct((C, M), F32),
            jax.ShapeDtypeStruct((16, C), F32),
            jax.ShapeDtypeStruct((1, 16), F32),
        ],
        in_specs=[in_hbm] * 6,
        out_specs=[in_hbm] * 4,
        scratch_shapes=[
            vmem(2, PG, C),
            vmem(2, PG, C),
            vmem(40, M),
            vmem(C, M),
            pltpu.VMEM((PG, M), BF16),
            vmem(32, C),
            vmem(SC, 8, C),
            vmem(S, C, M),
            vmem(C, M),
            vmem(1, 16),
            dma((7,)),
            dma((4,)),
        ],
        compiler_params=pltpu.CompilerParams(vmem_limit_bytes=VMEM_LIMIT),
        name="outputs",
    )(*between)
    return occupancy, account_value, credited.T, value.reshape(16)


def solution(mesh):
    placed = (
        P("mp"),
        P("mp"),
        P("mp"),
        P(),
        P(),
        P(),
        P("mp", None),
        P("mp", None),
        P("mp"),
        P("scen"),
        P(None, "scen"),
        P(),
        P(),
        P("scen", None),
    )
    return jax.shard_map(
        body,
        mesh=mesh,
        in_specs=placed,
        out_specs=(P(None, "scen", "mp"), P("scen", "mp"), P("scen", "mp"), P("mp")),
        check_vma=False,
    )
```

```python
import functools

import jax
import jax.numpy as jnp
from jax import lax
from jax.experimental import pallas as pl
from jax.experimental.pallas import tpu as pltpu
from jax.sharding import PartitionSpec as P

MESH = pl.DeviceIdType.MESH
EXACT = lax.Precision.HIGHEST
F32, BF16 = jnp.float32, jnp.bfloat16
STAY_WEIGHT = 40.0
LAPSE_SLOPE = 30.0
LIQUID_CHARGE = 0.5

S = 8
PG = 256
K = 256
DATES = 4
MONTHS = 3
C = 128
M = 1024
B = 2560
TILE = 256
MP = 16
SC = 16
SCEN = C * SC
KD = K // SC
GQ = 2 * PG // MP
VMEM_LIMIT = 56 * 1024 * 1024

NT = (((1,), (1,)), ((), ()))
NN = (((1,), (0,)), ((), ()))


def dot(a, b, dims, precision=None):
    return lax.dot_general(a, b, dims, precision=precision, preferred_element_type=F32)


def parts(x, count):
    found = []
    for _ in range(count):
        found.append(x.astype(BF16))
        x = x - found[-1].astype(F32)
    return found


def stack_parts(x, count, rows):
    found = parts(x, count)
    pieces = [piece.astype(F32) for piece in found]
    rest = rows - count * x.shape[0]
    if rest:
        pieces.append(jnp.zeros((rest, x.shape[1]), F32))
    return jnp.concatenate(pieces, axis=0).astype(BF16)


def iota(shape, axis):
    return lax.broadcasted_iota(jnp.int32, shape, axis)


def group_at(place):
    block = place // 16
    return (block // 4 * 4 + block % 2 * 2 + block // 2 % 2) * 16 + place % 16


def swap_blocks(rows):
    block = iota(rows.shape, 1) // 16 % 4
    width = rows.shape[1]
    up = pltpu.roll(rows, width - 16, 1)
    down = pltpu.roll(rows, 16, 1)
    return jnp.where(block == 1, up, jnp.where(block == 2, down, rows))


def discounts(rates, date):
    horizon = iota((K, C), 0)
    tenor = (horizon - date + 1).astype(F32) / 12.0
    factor = jnp.exp(-tenor * rates[date : date + 1, :])
    return jnp.where(horizon >= date, factor, 0.0) if date else factor


def exchange_kernel(
    base_hbm,
    moves_hbm,
    block_hbm,
    flows_hbm,
    group_hbm,
    state_hbm,
    account_hbm,
    transition_hbm,
    benefit_hbm,
    guarantee_hbm,
    spread_hbm,
    lapse_hbm,
    target_hbm,
    start_hbm,
    rho_hbm,
    pre_hbm,
    table_hbm,
    lapse1_hbm,
    small_hbm,
    value_hbm,
    pre_ref,
    table_ref,
    lapse1_ref,
    small_ref,
    base_ref,
    moves_ref,
    block_ref,
    flows_ref,
    group_ref,
    state_ref,
    account_ref,
    transition_ref,
    benefit_ref,
    guarantee_ref,
    spread_ref,
    lapse_ref,
    target_ref,
    start_ref,
    flow_parts,
    chosen_ref,
    bond_ref,
    point_ref,
    disc_ref,
    cols_ref,
    first_ref,
    a_src,
    a_buf,
    e_src,
    e_buf,
    b_src,
    b_buf,
    c_buf,
    d_src,
    f_src,
    load_sem,
    a_sems,
    b_sems,
    c_sems,
    d_first_sems,
    d_second_sems,
    e_sems,
    f_sems,
):
    d_sems = [d_first_sems, d_second_sems]
    mp, sc = lax.axis_index("mp"), lax.axis_index("scen")
    x, zh, core = mp // 4, mp // 2 % 2, mp % 2
    own = x * 2 + core
    zl, y = sc // 4, sc % 4

    def mp_index(dx, dz, dc):
        return (x + dx) % 4 * 4 + (zh + dz) % 2 * 2 + (core + dc) % 2

    def months_of(scen, half):
        return (scen // 4 + 2 * half) % 4 * 4 + scen % 4

    def scen_peer(dz, dy):
        there = (zl + dz) % 4
        across = (there - zl) * (there - zl) // 9
        return mp_index(0, across, 0), there * 4 + (y + dy) % 4

    steps = [(dz, dy) for dz in (2, 1, 3, 0) for dy in (2, 1, 3, 0) if (dz, dy) != (0, 0)]
    a_peers = [scen_peer(dz, dy) for dz, dy in steps]
    c_peers = [(mp, (zl + dz) % 4 * 4 + (y + dy) % 4) for dz, dy in steps]
    b_peers = [
        (mp_index(dx, dz, dc), (zl + 2 * dz) % 4 * 4 + y)
        for dz in (1, 0)
        for dx in (2, 1, 3, 0)
        for dc in (0, 1)
        if (dx, dz, dc) != (0, 0, 0)
    ]
    d_peers = [(mp_index(dx, 0, dc), sc) for dx in (2, 1, 3, 0) for dc in (0, 1) if (dx, dc) != (0, 0)]

    barrier = pltpu.get_barrier_semaphore()
    greeted = a_peers + b_peers
    for peer in greeted:
        pl.semaphore_signal(barrier, inc=1, device_id=peer, device_id_type=MESH)
    loads = [
        pltpu.make_async_copy(src, dst, load_sem.at[n])
        for n, (src, dst) in enumerate(
            [
                (base_hbm, base_ref),
                (moves_hbm, moves_ref),
                (block_hbm, block_ref),
                (flows_hbm, flows_ref),
                (group_hbm, group_ref),
                (state_hbm, state_ref),
                (account_hbm, account_ref),
                (transition_hbm, transition_ref),
                (benefit_hbm, benefit_ref),
                (guarantee_hbm, guarantee_ref),
                (spread_hbm, spread_ref),
                (lapse_hbm, lapse_ref),
                (target_hbm, target_ref),
                (start_hbm, start_ref),
            ]
        )
    ]
    for load in loads:
        load.start()

    def send_to(peers, src, dst, sems):
        for peer in peers:
            pltpu.make_async_remote_copy(
                src_ref=src(peer), dst_ref=dst, send_sem=sems.at[0], recv_sem=sems.at[1],
                device_id=peer, device_id_type=MESH,
            ).start()

    def all_of(peers, span, sems):
        return pltpu.make_async_remote_copy(
            src_ref=span, dst_ref=span, send_sem=sems.at[0], recv_sem=sems.at[1],
            device_id=peers[0], device_id_type=MESH,
        )

    def pair(peer):
        return peer[0] // 4 * 2 + peer[0] % 2

    a_all = all_of(a_peers, a_buf.at[: SC - 1], a_sems)
    b_all = all_of(b_peers, b_buf.at[: MP - 1], b_sems)
    c_all = all_of(c_peers, c_buf.at[: K - KD], c_sems)
    d_alls = [all_of(d_peers, rho_hbm.at[month, : PG - GQ], d_sems[month]) for month in range(MONTHS - 1)]
    e_all = all_of(b_peers, e_buf.at[: MP - 1], e_sems)
    f_all = all_of(a_peers, value_hbm.at[: SC - 1], f_sems)
    months = months_of(sc, zh)

    for load in loads[:2]:
        load.wait()
    rates = [base_ref[...]]
    for month in range(MONTHS):
        rates.append(rates[-1] + moves_ref[month : month + 1, :])
    rates = jnp.concatenate(rates, axis=0)
    blank = jnp.zeros((8, C), F32)
    small_ref[16:32, :] = jnp.concatenate([blank, rates, blank[:4]], axis=0)
    ones = jnp.ones((16, C), BF16)
    sums = []
    for date in range(DATES):
        pieces = parts(discounts(rates, date), 3)
        total = jnp.zeros((16, K), F32)
        for number, piece in enumerate(pieces):
            disc_ref[date, number] = piece
        for piece in reversed(pieces):
            total = total + dot(ones, piece, NT)
        sums.append(total[0:1])
    sums = jnp.concatenate(sums, axis=0)
    a_src[...] = jnp.concatenate([sums[:, : K // 2], sums[:, K // 2 :]], axis=0)

    pl.semaphore_wait(barrier, len(greeted))
    send_to(a_peers, lambda peer: a_src, a_buf.at[sc], a_sems)
    a_buf[sc] = a_src[...]

    for load in loads[2:4]:
        load.wait()
    picks = iota((32, K), 0)
    wanted = jnp.where(picks < KD, months * KD + picks, picks - KD)
    chosen = ((iota((32, K), 1) == wanted) & (picks < KD + MONTHS)).astype(BF16)
    bond_labels = group_at(iota((PG, TILE), 0))

    def prepare(tile, income):
        at = pl.ds(pl.multiple_of(tile * TILE, TILE), TILE)
        pieces = parts(flows_ref[at, :], 3)
        for number in range(2):
            flow_parts[number, :, at] = jnp.transpose(pieces[number])
        found = dot(chosen, pieces[2], NT) + dot(chosen, pieces[1], NT) + dot(chosen, pieces[0], NT)
        chosen_ref[:, at] = found[:KD]
        groups = (bond_labels == block_ref[:, at]).astype(BF16)
        bond_ref[:, at] = groups
        return income + dot(stack_parts(found[KD : KD + 8], 3, 32), groups, NT)

    income = lax.fori_loop(0, B // TILE, prepare, jnp.zeros((32, PG), F32), unroll=2)
    income = income[0:8] + income[8:16] + income[16:24]

    for load in loads[4:]:
        load.wait()
    accounts = jnp.zeros((32, PG), F32)
    for tile in range(M // TILE):
        at = pl.ds(tile * TILE, TILE)
        groups = (bond_labels == group_ref[:, at]).astype(BF16)
        point_ref[:, at] = groups
        mass = jnp.where(iota((S, TILE), 0) == state_ref[:, at], account_ref[:, at], 0.0)
        accounts = accounts + dot(stack_parts(mass, 3, 32), groups, NT)
    accounts = accounts[0:8] + accounts[8:16] + accounts[16:24]

    move = []
    for s in range(S):
        row = transition_ref[s] + jnp.where(iota((S, PG), 0) == s, STAY_WEIGHT, 0.0)
        move.append(row / jnp.sum(row, axis=0, keepdims=True))
    powers = [move]
    for _ in range(MONTHS - 1):
        last = powers[-1]
        powers.append([functools.reduce(jnp.add, [last[s][v : v + 1] * move[v] for v in range(S)]) for s in range(S)])
    benefit = jnp.where(iota((S, S), 0) == iota((S, S), 1), benefit_ref[...], 0.0)
    benefit = jnp.sum(benefit, axis=1, keepdims=True)
    stays = [jnp.concatenate([power[s][0:1] for s in range(S)], axis=0) for power in powers]
    pays = [
        jnp.concatenate([jnp.sum(power[s] * benefit, axis=0, keepdims=True) for s in range(S)], axis=0)
        for power in powers
    ]

    def by_state(rows):
        return jnp.sum(accounts * swap_blocks(rows), axis=0, keepdims=True)

    early = [accounts[0:1], by_state(stays[0]), by_state(stays[1]), by_state(pays[0]), by_state(pays[1]), by_state(pays[2])]
    early = jnp.concatenate(early + [jnp.zeros((2, PG), F32)], axis=0)
    for q in range(MP // 2):
        e_src[q] = jnp.concatenate(
            [early[:, q * GQ : (q + 1) * GQ], income[:, q * GQ : (q + 1) * GQ], jnp.zeros((8, C - 2 * GQ), F32)], axis=1
        )
    send_to(b_peers, lambda peer: e_src.at[pair(peer)], e_buf.at[mp], e_sems)
    e_buf[mp] = e_src[own]

    a_all.wait_recv()
    mean = a_buf[0]
    for slot in range(1, SC):
        mean = mean + a_buf[slot]
    mean = mean * (1.0 / SCEN)
    mean = stack_parts(jnp.concatenate([mean[0:4], mean[4:8]], axis=1), 3, 16)

    def weigh(tile, total):
        at = pl.ds(pl.multiple_of(tile * TILE, TILE), TILE)
        high = dot(mean, flow_parts[0, :, at], NN)
        middle = dot(mean, flow_parts[1, :, at], NN)
        price = high[0:4] + ((high[4:8] + middle[0:4]) + (high[8:12] + middle[4:8]))
        target = [target_ref[pl.ds(tile * 2 + n, 1), :] for n in range(2)]
        weight = jnp.concatenate(target, axis=1) / price
        flows = chosen_ref[:, at]
        scaled = jnp.concatenate([weight[date : date + 1] * flows for date in range(DATES)], axis=0)
        return total + dot(stack_parts(scaled, 3, 3 * DATES * KD), bond_ref[:, at], NT)

    worth = lax.fori_loop(0, B // TILE, weigh, jnp.zeros((3 * DATES * KD, PG), F32), unroll=True)
    size = DATES * KD
    worth = worth[0:size] + (worth[size : 2 * size] + worth[2 * size :])
    for q in range(MP // 2):
        b_src[q] = jnp.concatenate(
            [worth[date * KD : (date + 1) * KD, q * GQ : (q + 1) * GQ] for date in range(DATES)], axis=1
        )
    send_to(b_peers, lambda peer: b_src.at[pair(peer)], b_buf.at[mp], b_sems)
    b_buf[mp] = b_src[own]

    local = [guarantee_ref[...], spread_ref[...], lapse_ref[...], stays[0][0:1], stays[1][0:1], pays[0][0:1], pays[1][0:1], pays[2][0:1]]
    local = jnp.concatenate(local, axis=0)
    order = (group_at(iota((PG, PG), 0)) == iota((PG, PG), 1)).astype(F32)
    cols_ref[...] = dot(order, local, NT, EXACT)
    first_ref[...] = dot(order, start_ref[...], NT, EXACT)
    twice = jnp.broadcast_to(cols_ref[:, 2:3] * 2.0, (PG, C))
    pre_ref[0] = twice
    pre_ref[1] = first_ref[...]
    start_lapse = twice * jax.nn.sigmoid(LAPSE_SLOPE * (rates[0:1] - first_ref[...]))
    start_lapse = stack_parts(jnp.transpose(start_lapse), 2, 2 * C)

    gathered = jnp.concatenate(powers[2] + [powers[1][0], powers[0][0], stays[1], stays[0]], axis=0)
    gathered = stack_parts(swap_blocks(gathered), 2, 192)
    for tile in range(M // TILE):
        at = pl.ds(tile * TILE, TILE)
        found = dot(gathered, point_ref[:, at], NN)
        found = found[0:96] + found[96:192]
        states = state_ref[:, at]
        last = jnp.zeros((S, TILE), F32)
        for s in range(S):
            last = jnp.where(states == s, found[s * S : (s + 1) * S], last)
        held = iota((S, TILE), 0) == states
        second = jnp.sum(jnp.where(held, found[80:88], 0.0), axis=0, keepdims=True)
        first = jnp.sum(jnp.where(held, found[88:96], 0.0), axis=0, keepdims=True)
        start = (states == 0).astype(F32)
        lapsed = dot(start_lapse, point_ref[:, at], NN)
        lapse1_ref[:, at] = (lapsed[:C] + lapsed[C:]) * start
        table_ref[0:8, at] = last
        table_ref[8:16, at] = found[0:8]
        table_ref[16:24, at] = found[64:72]
        table_ref[24:32, at] = found[72:80]
        table_ref[32:40, at] = jnp.concatenate(
            [start, first, second, account_ref[:, at], group_ref[:, at].astype(F32), jnp.zeros((3, TILE), F32)],
            axis=0,
        )
    stores = [
        pltpu.make_async_copy(src, dst, load_sem.at[n])
        for n, (src, dst) in enumerate(
            [
                (pre_ref, pre_hbm),
                (table_ref, table_hbm),
                (lapse1_ref, lapse1_hbm),
            ]
        )
    ]
    for store in stores:
        store.start()

    b_all.wait_recv()
    total = b_buf[0]
    for slot in range(1, MP):
        total = total + b_buf[slot]
    rows = pl.ds(pl.multiple_of(months * KD, KD), KD)
    c_buf[rows, :] = total
    send_to(c_peers, lambda peer: c_buf.at[rows, :], c_buf.at[rows, :], c_sems)

    e_all.wait_recv()
    early = e_buf[0]
    for slot in range(1, MP):
        early = early + e_buf[slot]
    early = jnp.transpose(jnp.concatenate([early, jnp.zeros((C - 8, C), F32)], axis=0))
    income = early[GQ : 2 * GQ]
    mine = pl.ds(pl.multiple_of(own * GQ, GQ), GQ)
    columns = cols_ref[mine, :]
    guarantee, spread, lapse_base = columns[:, 0:1], columns[:, 1:2], columns[:, 2:3]
    stay = [columns[:, 3:4], columns[:, 4:5]]
    pay = [columns[:, 5:6], columns[:, 6:7], columns[:, 7:8]]
    credited = first_ref[mine, :]

    c_all.wait_recv()
    worth = jnp.transpose(c_buf[...])

    def assets_at(date):
        pieces = stack_parts(worth[date * GQ : (date + 1) * GQ], 3, 3 * GQ)
        high = dot(pieces, disc_ref[date, 0], NN)
        middle = dot(pieces[: 2 * GQ], disc_ref[date, 1], NN)
        low = dot(pieces[:GQ], disc_ref[date, 2], NN)
        return high[:GQ] + ((high[GQ : 2 * GQ] + middle[:GQ]) + (high[2 * GQ :] + middle[GQ:] + low))

    growth = jnp.ones((GQ, C), F32)
    present = jnp.zeros((GQ, C), F32)
    lapses = []
    held = assets_at(0)
    for month in range(MONTHS):
        factor = lapse_base * 2.0 * jax.nn.sigmoid(LAPSE_SLOPE * (rates[month : month + 1] - credited))
        mass = early[:GQ, month : month + 1]
        for lag, lapse in enumerate(reversed(lapses)):
            mass = mass - lapse * stay[lag]
        lapses.append(mass * factor)
        growth = growth * (1.0 + credited / 12.0)
        paid = early[:GQ, 3 + month : 4 + month]
        for lag, lapse in enumerate(reversed(lapses)):
            paid = paid - lapse * pay[lag]
        flows = growth * (lapses[-1] + paid)
        after = assets_at(month + 1)
        later = after + income[:, month : month + 1]
        earned = 12.0 * (later - held) / held
        credited = jnp.maximum(
            guarantee, 0.5 * credited + 0.5 * (earned - spread) - LIQUID_CHARGE * flows / held
        )
        if month < MONTHS - 1:
            d_src[month] = credited
            send_to(d_peers, lambda peer: d_src.at[month], rho_hbm.at[month, mine, :], d_sems[month])
        held = after
        present = present + flows * jnp.exp(-rates[month + 1 : month + 2] * ((month + 1) / 12.0))
    sums = dot(jnp.ones((8, C), F32), jnp.concatenate([present, jnp.zeros((C - GQ, C), F32)], axis=0), NT, EXACT)
    f_src[0] = sums
    f_src[1] = pltpu.roll(sums, C - 16, 1)
    send_to(a_peers, lambda peer: f_src.at[peer[0] // 2 % 2], value_hbm.at[sc], f_sems)
    small_ref[0:16, :] = 100.0 * jnp.where(zh == 0, credited[:16], credited[16:])
    late = [
        pltpu.make_async_copy(src, dst, load_sem.at[4 + n])
        for n, (src, dst) in enumerate(
            [
                (small_ref, small_hbm),
                (f_src.at[zh], value_hbm.at[sc]),
                (d_src.at[0], rho_hbm.at[0, mine, :]),
                (d_src.at[1], rho_hbm.at[1, mine, :]),
            ]
        )
    ]
    for store in late:
        store.start()
    for exchange in (a_all, e_all, b_all, c_all):
        exchange.wait_send()
    for store in stores + late:
        store.wait()
    for exchange in (*d_alls, f_all):
        exchange.wait_send()
        exchange.wait_recv()


CHUNK = 16


def output_kernel(
    rho_hbm, pre_hbm, table_hbm, lapse1_hbm, small_hbm, value_hbm,
    occupancy_hbm, account_hbm, credited_hbm, out_value_hbm,
    rho_ref, pre_ref, table_ref, lapse1_ref, point_ref, small_ref, sums_ref,
    occupancy_ref, account_ref, value_ref, load_sem, store_sem,
):
    loads = [
        pltpu.make_async_copy(src, dst, load_sem.at[n])
        for n, (src, dst) in enumerate(
            [
                (table_hbm, table_ref),
                (rho_hbm, rho_ref),
                (pre_hbm, pre_ref),
                (small_hbm, small_ref),
                (lapse1_hbm.at[:CHUNK], lapse1_ref.at[:CHUNK]),
                (lapse1_hbm.at[CHUNK:], lapse1_ref.at[CHUNK:]),
                (value_hbm, sums_ref),
            ]
        )
    ]
    for load in loads:
        load.start()
    loads[0].wait()
    labels = group_at(iota((PG, TILE), 0)).astype(F32)
    for tile in range(M // TILE):
        at = pl.ds(tile * TILE, TILE)
        point_ref[:, at] = (labels == table_ref[36:37, at]).astype(BF16)
    for load in loads[1:4]:
        load.wait()
    copies = [pltpu.make_async_copy(small_ref.at[0:16, :], credited_hbm, store_sem.at[2])]
    copies[0].start()
    twice = pre_ref[0]
    rho = [pre_ref[1], rho_ref[0], rho_ref[1]]
    tables = []
    for month in (1, 2):
        rates = small_ref[24 + month : 25 + month, :]
        tables.append(twice * jax.nn.sigmoid(LAPSE_SLOPE * (rates - rho[month])))
    grown = [rate * (1.0 / 12.0) for rate in rho]
    gain = grown[0] + grown[1] + grown[0] * grown[1]
    tables.append(gain + grown[2] + gain * grown[2])
    tables = [parts(jnp.transpose(table), 2) for table in tables]

    loads[4].wait()
    for chunk in range(C // CHUNK):
        rows = slice(chunk * CHUNK, (chunk + 1) * CHUNK)
        lhs = jnp.concatenate([piece[rows] for table in tables for piece in table], axis=0)
        for tile in range(M // TILE):
            at = pl.ds(tile * TILE, TILE)
            found = dot(lhs, point_ref[:, at], NN)
            found = [
                found[2 * n * CHUNK : (2 * n + 1) * CHUNK] + found[(2 * n + 1) * CHUNK : (2 * n + 2) * CHUNK]
                for n in range(3)
            ]
            first = lapse1_ref[rows, at]
            second = (table_ref[33:34, at] - first * table_ref[24:25, at]) * found[0]
            third = (table_ref[34:35, at] - first * table_ref[16:17, at] - second * table_ref[24:25, at]) * found[1]
            for u in range(S):
                occupancy_ref[u, rows, at] = (
                    table_ref[u : u + 1, at]
                    - first * table_ref[8 + u : 9 + u, at]
                    - second * table_ref[16 + u : 17 + u, at]
                    - third * table_ref[24 + u : 25 + u, at]
                )
            account = table_ref[35:36, at]
            account_ref[rows, at] = account + account * found[2]
        pltpu.make_async_copy(occupancy_ref.at[:, rows, :], occupancy_hbm.at[:, rows, :], store_sem.at[0]).start()
        pltpu.make_async_copy(account_ref.at[rows, :], account_hbm.at[rows, :], store_sem.at[1]).start()
        if chunk == 0:
            for load in loads[5:]:
                load.wait()
            value = sums_ref[0]
            for slot in range(1, SC):
                value = value + sums_ref[slot]
            value_ref[...] = value[0:1, 0:16] * (1.0 / SCEN)
            copies.append(pltpu.make_async_copy(value_ref, out_value_hbm, store_sem.at[3]))
            copies[-1].start()
    copies.append(pltpu.make_async_copy(occupancy_ref, occupancy_hbm, store_sem.at[0]))
    copies.append(pltpu.make_async_copy(account_ref, account_hbm, store_sem.at[1]))
    for copy in copies:
        copy.wait()


def vmem(*shape):
    return pltpu.VMEM(shape, F32)


def body(
    group_id,
    issue_state,
    account_start,
    transition,
    lapse_base,
    benefit,
    bond_block,
    bond_flows,
    bond_target,
    base_rate,
    rate_moves,
    guarantee,
    spread,
    start_rate,
):
    in_hbm = pl.BlockSpec(memory_space=pltpu.HBM)
    dma = pltpu.SemaphoreType.DMA
    between = pl.pallas_call(
        exchange_kernel,
        out_shape=[
            jax.ShapeDtypeStruct((2, PG, C), F32),
            jax.ShapeDtypeStruct((2, PG, C), F32),
            jax.ShapeDtypeStruct((40, M), F32),
            jax.ShapeDtypeStruct((C, M), F32),
            jax.ShapeDtypeStruct((32, C), F32),
            jax.ShapeDtypeStruct((SC, 8, C), F32),
        ],
        in_specs=[in_hbm] * 14,
        out_specs=[in_hbm] * 6,
        scratch_shapes=[
            vmem(2, PG, C),
            vmem(40, M),
            vmem(C, M),
            vmem(32, C),
            vmem(1, C),
            vmem(MONTHS, C),
            pltpu.VMEM((1, B), jnp.int32),
            vmem(B, K),
            pltpu.VMEM((1, M), jnp.int32),
            pltpu.VMEM((1, M), jnp.int32),
            vmem(1, M),
            vmem(S, S, PG),
            vmem(1, S),
            vmem(1, PG),
            vmem(1, PG),
            vmem(1, PG),
            vmem(B // C, C),
            vmem(C, PG),
            pltpu.VMEM((2, K, B), BF16),
            vmem(KD, B),
            pltpu.VMEM((PG, B), BF16),
            pltpu.VMEM((PG, M), BF16),
            pltpu.VMEM((DATES, 3, K, C), BF16),
            vmem(PG, 8),
            vmem(PG, C),
            vmem(8, C),
            vmem(SC, 8, C),
            vmem(MP // 2, 8, C),
            vmem(MP, 8, C),
            vmem(MP // 2, KD, C),
            vmem(MP, KD, C),
            vmem(K, C),
            vmem(2, GQ, C),
            vmem(2, 8, C),
            dma((14,)),
            *[dma((2,)) for _ in range(7)],
        ],
        compiler_params=pltpu.CompilerParams(
            collective_id=0, has_side_effects=True, vmem_limit_bytes=VMEM_LIMIT
        ),
        name="exchange",
    )(
        base_rate.reshape(1, C),
        rate_moves,
        bond_block.reshape(1, B),
        bond_flows,
        group_id.reshape(1, M),
        issue_state.reshape(1, M),
        account_start.reshape(1, M),
        transition.transpose(1, 2, 0),
        benefit.reshape(1, S),
        guarantee.reshape(1, PG),
        spread.reshape(1, PG),
        lapse_base.reshape(1, PG),
        bond_target.reshape(B // C, C),
        start_rate,
    )
    occupancy, account_value, credited, value = pl.pallas_call(
        output_kernel,
        out_shape=[
            jax.ShapeDtypeStruct((S, C, M), F32),
            jax.ShapeDtypeStruct((C, M), F32),
            jax.ShapeDtypeStruct((16, C), F32),
            jax.ShapeDtypeStruct((1, 16), F32),
        ],
        in_specs=[in_hbm] * 6,
        out_specs=[in_hbm] * 4,
        scratch_shapes=[
            vmem(2, PG, C),
            vmem(2, PG, C),
            vmem(40, M),
            vmem(C, M),
            pltpu.VMEM((PG, M), BF16),
            vmem(32, C),
            vmem(SC, 8, C),
            vmem(S, C, M),
            vmem(C, M),
            vmem(1, 16),
            dma((7,)),
            dma((4,)),
        ],
        compiler_params=pltpu.CompilerParams(vmem_limit_bytes=VMEM_LIMIT),
        name="outputs",
    )(*between)
    return occupancy, account_value, credited.T, value.reshape(16)


def solution(mesh):
    placed = (
        P("mp"),
        P("mp"),
        P("mp"),
        P(),
        P(),
        P(),
        P("mp", None),
        P("mp", None),
        P("mp"),
        P("scen"),
        P(None, "scen"),
        P(),
        P(),
        P("scen", None),
    )
    return jax.shard_map(
        body,
        mesh=mesh,
        in_specs=placed,
        out_specs=(P(None, "scen", "mp"), P("scen", "mp"), P("scen", "mp"), P("mp")),
        check_vma=False,
    )
```

```python
import functools

import jax
import jax.numpy as jnp
from jax import lax
from jax.experimental import pallas as pl
from jax.experimental.pallas import tpu as pltpu
from jax.sharding import PartitionSpec as P

MESH = pl.DeviceIdType.MESH
EXACT = lax.Precision.HIGHEST
F32, BF16 = jnp.float32, jnp.bfloat16
STAY_WEIGHT = 40.0
LAPSE_SLOPE = 30.0
LIQUID_CHARGE = 0.5

S = 8
PG = 256
K = 256
DATES = 4
MONTHS = 3
C = 128
M = 1024
B = 2560
TILE = 256
MP = 16
SC = 16
SCEN = C * SC
KD = K // SC
GQ = 2 * PG // MP
VMEM_LIMIT = 56 * 1024 * 1024

NT = (((1,), (1,)), ((), ()))
NN = (((1,), (0,)), ((), ()))


def dot(a, b, dims, precision=None):
    return lax.dot_general(a, b, dims, precision=precision, preferred_element_type=F32)


def parts(x, count):
    found = []
    for _ in range(count):
        found.append(x.astype(BF16))
        x = x - found[-1].astype(F32)
    return found


def stack_parts(x, count, rows):
    found = parts(x, count)
    pieces = [piece.astype(F32) for piece in found]
    rest = rows - count * x.shape[0]
    if rest:
        pieces.append(jnp.zeros((rest, x.shape[1]), F32))
    return jnp.concatenate(pieces, axis=0).astype(BF16)


def iota(shape, axis):
    return lax.broadcasted_iota(jnp.int32, shape, axis)


def group_at(place):
    block = place // 16
    return (block // 4 * 4 + block % 2 * 2 + block // 2 % 2) * 16 + place % 16


def swap_blocks(rows):
    block = iota(rows.shape, 1) // 16 % 4
    width = rows.shape[1]
    up = pltpu.roll(rows, width - 16, 1)
    down = pltpu.roll(rows, 16, 1)
    return jnp.where(block == 1, up, jnp.where(block == 2, down, rows))


def discounts(rates, date):
    horizon = iota((K, C), 0)
    tenor = (horizon - date + 1).astype(F32) / 12.0
    factor = jnp.exp(-tenor * rates[date : date + 1, :])
    return jnp.where(horizon >= date, factor, 0.0) if date else factor


def exchange_kernel(
    base_hbm,
    moves_hbm,
    block_hbm,
    flows_hbm,
    group_hbm,
    state_hbm,
    account_hbm,
    transition_hbm,
    benefit_hbm,
    guarantee_hbm,
    spread_hbm,
    lapse_hbm,
    target_hbm,
    start_hbm,
    rho_hbm,
    pre_hbm,
    table_hbm,
    lapse1_hbm,
    small_hbm,
    value_hbm,
    pre_ref,
    table_ref,
    lapse1_ref,
    small_ref,
    base_ref,
    moves_ref,
    block_ref,
    flows_ref,
    group_ref,
    state_ref,
    account_ref,
    transition_ref,
    benefit_ref,
    guarantee_ref,
    spread_ref,
    lapse_ref,
    target_ref,
    start_ref,
    flow_parts,
    chosen_ref,
    bond_ref,
    point_ref,
    disc_ref,
    cols_ref,
    first_ref,
    a_src,
    a_buf,
    e_src,
    e_buf,
    b_src,
    b_buf,
    c_buf,
    d_src,
    f_src,
    load_sem,
    a_sems,
    b_sems,
    c_sems,
    d_first_sems,
    d_second_sems,
    e_sems,
    f_sems,
):
    d_sems = [d_first_sems, d_second_sems]
    mp, sc = lax.axis_index("mp"), lax.axis_index("scen")
    x, zh, core = mp // 4, mp // 2 % 2, mp % 2
    own = x * 2 + core
    zl, y = sc // 4, sc % 4

    def mp_index(dx, dz, dc):
        return (x + dx) % 4 * 4 + (zh + dz) % 2 * 2 + (core + dc) % 2

    def months_of(scen, half):
        return (scen // 4 + 2 * half) % 4 * 4 + scen % 4

    def scen_peer(dz, dy):
        there = (zl + dz) % 4
        across = (there - zl) * (there - zl) // 9
        return mp_index(0, across, 0), there * 4 + (y + dy) % 4

    steps = [(dz, dy) for dz in (2, 1, 3, 0) for dy in (2, 1, 3, 0) if (dz, dy) != (0, 0)]
    a_peers = [scen_peer(dz, dy) for dz, dy in steps]
    c_peers = [(mp, (zl + dz) % 4 * 4 + (y + dy) % 4) for dz, dy in steps]
    b_peers = [
        (mp_index(dx, dz, dc), (zl + 2 * dz) % 4 * 4 + y)
        for dz in (1, 0)
        for dx in (2, 1, 3, 0)
        for dc in (0, 1)
        if (dx, dz, dc) != (0, 0, 0)
    ]
    d_peers = [(mp_index(dx, 0, dc), sc) for dx in (2, 1, 3, 0) for dc in (0, 1) if (dx, dc) != (0, 0)]

    barrier = pltpu.get_barrier_semaphore()
    greeted = a_peers + b_peers
    for peer in greeted:
        pl.semaphore_signal(barrier, inc=1, device_id=peer, device_id_type=MESH)
    loads = [
        pltpu.make_async_copy(src, dst, load_sem.at[n])
        for n, (src, dst) in enumerate(
            [
                (base_hbm, base_ref),
                (moves_hbm, moves_ref),
                (block_hbm, block_ref),
                (flows_hbm, flows_ref),
                (group_hbm, group_ref),
                (state_hbm, state_ref),
                (account_hbm, account_ref),
                (transition_hbm, transition_ref),
                (benefit_hbm, benefit_ref),
                (guarantee_hbm, guarantee_ref),
                (spread_hbm, spread_ref),
                (lapse_hbm, lapse_ref),
                (target_hbm, target_ref),
                (start_hbm, start_ref),
            ]
        )
    ]
    for load in loads:
        load.start()

    def send_to(peers, src, dst, sems):
        for peer in peers:
            pltpu.make_async_remote_copy(
                src_ref=src(peer), dst_ref=dst, send_sem=sems.at[0], recv_sem=sems.at[1],
                device_id=peer, device_id_type=MESH,
            ).start()

    def all_of(peers, span, sems):
        return pltpu.make_async_remote_copy(
            src_ref=span, dst_ref=span, send_sem=sems.at[0], recv_sem=sems.at[1],
            device_id=peers[0], device_id_type=MESH,
        )

    def pair(peer):
        return peer[0] // 4 * 2 + peer[0] % 2

    a_all = all_of(a_peers, a_buf.at[: SC - 1], a_sems)
    b_all = all_of(b_peers, b_buf.at[: MP - 1], b_sems)
    c_all = all_of(c_peers, c_buf.at[: K - KD], c_sems)
    d_alls = [all_of(d_peers, rho_hbm.at[month, : PG - GQ], d_sems[month]) for month in range(MONTHS - 1)]
    e_all = all_of(b_peers, e_buf.at[: MP - 1], e_sems)
    f_all = all_of(a_peers, value_hbm.at[: SC - 1], f_sems)
    months = months_of(sc, zh)

    for load in loads[:2]:
        load.wait()
    rates = [base_ref[...]]
    for month in range(MONTHS):
        rates.append(rates[-1] + moves_ref[month : month + 1, :])
    rates = jnp.concatenate(rates, axis=0)
    blank = jnp.zeros((8, C), F32)
    small_ref[16:32, :] = jnp.concatenate([blank, rates, blank[:4]], axis=0)
    ones = jnp.ones((16, C), BF16)
    sums = []
    for date in range(DATES):
        pieces = parts(discounts(rates, date), 3)
        total = jnp.zeros((16, K), F32)
        for number, piece in enumerate(pieces):
            disc_ref[date, number] = piece
        for piece in reversed(pieces):
            total = total + dot(ones, piece, NT)
        sums.append(total[0:1])
    sums = jnp.concatenate(sums, axis=0)
    a_src[...] = jnp.concatenate([sums[:, : K // 2], sums[:, K // 2 :]], axis=0)

    pl.semaphore_wait(barrier, len(greeted))
    send_to(a_peers, lambda peer: a_src, a_buf.at[sc], a_sems)
    a_buf[sc] = a_src[...]

    for load in loads[2:4]:
        load.wait()
    picks = iota((32, K), 0)
    wanted = jnp.where(picks < KD, months * KD + picks, picks - KD)
    chosen = ((iota((32, K), 1) == wanted) & (picks < KD + MONTHS)).astype(BF16)
    bond_labels = group_at(iota((PG, TILE), 0))

    def prepare(tile, income):
        at = pl.ds(pl.multiple_of(tile * TILE, TILE), TILE)
        pieces = parts(flows_ref[at, :], 3)
        for number in range(2):
            flow_parts[number, :, at] = jnp.transpose(pieces[number])
        found = dot(chosen, pieces[2], NT) + dot(chosen, pieces[1], NT) + dot(chosen, pieces[0], NT)
        chosen_ref[:, at] = found[:KD]
        groups = (bond_labels == block_ref[:, at]).astype(BF16)
        bond_ref[:, at] = groups
        return income + dot(stack_parts(found[KD : KD + 8], 3, 32), groups, NT)

    income = lax.fori_loop(0, B // TILE, prepare, jnp.zeros((32, PG), F32), unroll=2)
    income = income[0:8] + income[8:16] + income[16:24]

    for load in loads[4:]:
        load.wait()
    accounts = jnp.zeros((32, PG), F32)
    for tile in range(M // TILE):
        at = pl.ds(tile * TILE, TILE)
        groups = (bond_labels == group_ref[:, at]).astype(BF16)
        point_ref[:, at] = groups
        mass = jnp.where(iota((S, TILE), 0) == state_ref[:, at], account_ref[:, at], 0.0)
        accounts = accounts + dot(stack_parts(mass, 3, 32), groups, NT)
    accounts = accounts[0:8] + accounts[8:16] + accounts[16:24]

    move = []
    for s in range(S):
        row = transition_ref[s] + jnp.where(iota((S, PG), 0) == s, STAY_WEIGHT, 0.0)
        move.append(row / jnp.sum(row, axis=0, keepdims=True))
    powers = [move]
    for _ in range(MONTHS - 1):
        last = powers[-1]
        powers.append([functools.reduce(jnp.add, [last[s][v : v + 1] * move[v] for v in range(S)]) for s in range(S)])
    benefit = jnp.where(iota((S, S), 0) == iota((S, S), 1), benefit_ref[...], 0.0)
    benefit = jnp.sum(benefit, axis=1, keepdims=True)
    stays = [jnp.concatenate([power[s][0:1] for s in range(S)], axis=0) for power in powers]
    pays = [
        jnp.concatenate([jnp.sum(power[s] * benefit, axis=0, keepdims=True) for s in range(S)], axis=0)
        for power in powers
    ]

    def by_state(rows):
        return jnp.sum(accounts * swap_blocks(rows), axis=0, keepdims=True)

    early = [accounts[0:1], by_state(stays[0]), by_state(stays[1]), by_state(pays[0]), by_state(pays[1]), by_state(pays[2])]
    early = jnp.concatenate(early + [jnp.zeros((2, PG), F32)], axis=0)
    for q in range(MP // 2):
        e_src[q] = jnp.concatenate(
            [early[:, q * GQ : (q + 1) * GQ], income[:, q * GQ : (q + 1) * GQ], jnp.zeros((8, C - 2 * GQ), F32)], axis=1
        )
    e_buf[mp] = e_src[own]

    a_all.wait_recv()
    mean = a_buf[0]
    for slot in range(1, SC):
        mean = mean + a_buf[slot]
    mean = mean * (1.0 / SCEN)
    mean = stack_parts(jnp.concatenate([mean[0:4], mean[4:8]], axis=1), 3, 16)

    def weigh(tile, total):
        at = pl.ds(pl.multiple_of(tile * TILE, TILE), TILE)
        high = dot(mean, flow_parts[0, :, at], NN)
        middle = dot(mean, flow_parts[1, :, at], NN)
        price = high[0:4] + ((high[4:8] + middle[0:4]) + (high[8:12] + middle[4:8]))
        target = [target_ref[pl.ds(tile * 2 + n, 1), :] for n in range(2)]
        weight = jnp.concatenate(target, axis=1) / price
        flows = chosen_ref[:, at]
        scaled = jnp.concatenate([weight[date : date + 1] * flows for date in range(DATES)], axis=0)
        return total + dot(stack_parts(scaled, 3, 3 * DATES * KD), bond_ref[:, at], NT)

    worth = lax.fori_loop(0, B // TILE, weigh, jnp.zeros((3 * DATES * KD, PG), F32), unroll=True)
    size = DATES * KD
    worth = worth[0:size] + (worth[size : 2 * size] + worth[2 * size :])
    for q in range(MP // 2):
        b_src[q] = jnp.concatenate(
            [worth[date * KD : (date + 1) * KD, q * GQ : (q + 1) * GQ] for date in range(DATES)], axis=1
        )
    send_to(b_peers, lambda peer: b_src.at[pair(peer)], b_buf.at[mp], b_sems)
    send_to(b_peers, lambda peer: e_src.at[pair(peer)], e_buf.at[mp], e_sems)
    b_buf[mp] = b_src[own]

    local = [guarantee_ref[...], spread_ref[...], lapse_ref[...], stays[0][0:1], stays[1][0:1], pays[0][0:1], pays[1][0:1], pays[2][0:1]]
    local = jnp.concatenate(local, axis=0)
    order = (group_at(iota((PG, PG), 0)) == iota((PG, PG), 1)).astype(F32)
    cols_ref[...] = dot(order, local, NT, EXACT)
    first_ref[...] = dot(order, start_ref[...], NT, EXACT)
    twice = jnp.broadcast_to(cols_ref[:, 2:3] * 2.0, (PG, C))
    pre_ref[0] = twice
    pre_ref[1] = first_ref[...]
    start_lapse = twice * jax.nn.sigmoid(LAPSE_SLOPE * (rates[0:1] - first_ref[...]))
    start_lapse = stack_parts(jnp.transpose(start_lapse), 2, 2 * C)

    gathered = jnp.concatenate(powers[2] + [powers[1][0], powers[0][0], stays[1], stays[0]], axis=0)
    gathered = stack_parts(swap_blocks(gathered), 2, 192)
    for tile in range(M // TILE):
        at = pl.ds(tile * TILE, TILE)
        found = dot(gathered, point_ref[:, at], NN)
        found = found[0:96] + found[96:192]
        states = state_ref[:, at]
        last = jnp.zeros((S, TILE), F32)
        for s in range(S):
            last = jnp.where(states == s, found[s * S : (s + 1) * S], last)
        held = iota((S, TILE), 0) == states
        second = jnp.sum(jnp.where(held, found[80:88], 0.0), axis=0, keepdims=True)
        first = jnp.sum(jnp.where(held, found[88:96], 0.0), axis=0, keepdims=True)
        start = (states == 0).astype(F32)
        lapsed = dot(start_lapse, point_ref[:, at], NN)
        lapse1_ref[:, at] = (lapsed[:C] + lapsed[C:]) * start
        table_ref[0:8, at] = last
        table_ref[8:16, at] = found[0:8]
        table_ref[16:24, at] = found[64:72]
        table_ref[24:32, at] = found[72:80]
        table_ref[32:40, at] = jnp.concatenate(
            [start, first, second, account_ref[:, at], group_ref[:, at].astype(F32), jnp.zeros((3, TILE), F32)],
            axis=0,
        )
    stores = [
        pltpu.make_async_copy(src, dst, load_sem.at[n])
        for n, (src, dst) in enumerate(
            [
                (pre_ref, pre_hbm),
                (table_ref, table_hbm),
                (lapse1_ref, lapse1_hbm),
            ]
        )
    ]
    for store in stores:
        store.start()

    b_all.wait_recv()
    total = b_buf[0]
    for slot in range(1, MP):
        total = total + b_buf[slot]
    rows = pl.ds(pl.multiple_of(months * KD, KD), KD)
    c_buf[rows, :] = total
    send_to(c_peers, lambda peer: c_buf.at[rows, :], c_buf.at[rows, :], c_sems)

    e_all.wait_recv()
    early = e_buf[0]
    for slot in range(1, MP):
        early = early + e_buf[slot]
    early = jnp.transpose(jnp.concatenate([early, jnp.zeros((C - 8, C), F32)], axis=0))
    income = early[GQ : 2 * GQ]
    mine = pl.ds(pl.multiple_of(own * GQ, GQ), GQ)
    columns = cols_ref[mine, :]
    guarantee, spread, lapse_base = columns[:, 0:1], columns[:, 1:2], columns[:, 2:3]
    stay = [columns[:, 3:4], columns[:, 4:5]]
    pay = [columns[:, 5:6], columns[:, 6:7], columns[:, 7:8]]
    credited = first_ref[mine, :]

    c_all.wait_recv()
    worth = jnp.transpose(c_buf[...])

    def assets_at(date):
        pieces = stack_parts(worth[date * GQ : (date + 1) * GQ], 3, 3 * GQ)
        high = dot(pieces, disc_ref[date, 0], NN)
        middle = dot(pieces[: 2 * GQ], disc_ref[date, 1], NN)
        low = dot(pieces[:GQ], disc_ref[date, 2], NN)
        return high[:GQ] + ((high[GQ : 2 * GQ] + middle[:GQ]) + (high[2 * GQ :] + middle[GQ:] + low))

    growth = jnp.ones((GQ, C), F32)
    present = jnp.zeros((GQ, C), F32)
    lapses = []
    held = assets_at(0)
    for month in range(MONTHS):
        factor = lapse_base * 2.0 * jax.nn.sigmoid(LAPSE_SLOPE * (rates[month : month + 1] - credited))
        mass = early[:GQ, month : month + 1]
        for lag, lapse in enumerate(reversed(lapses)):
            mass = mass - lapse * stay[lag]
        lapses.append(mass * factor)
        growth = growth * (1.0 + credited / 12.0)
        paid = early[:GQ, 3 + month : 4 + month]
        for lag, lapse in enumerate(reversed(lapses)):
            paid = paid - lapse * pay[lag]
        flows = growth * (lapses[-1] + paid)
        after = assets_at(month + 1)
        later = after + income[:, month : month + 1]
        earned = 12.0 * (later - held) / held
        credited = jnp.maximum(
            guarantee, 0.5 * credited + 0.5 * (earned - spread) - LIQUID_CHARGE * flows / held
        )
        if month < MONTHS - 1:
            d_src[month] = credited
            send_to(d_peers, lambda peer: d_src.at[month], rho_hbm.at[month, mine, :], d_sems[month])
        held = after
        present = present + flows * jnp.exp(-rates[month + 1 : month + 2] * ((month + 1) / 12.0))
    sums = dot(jnp.ones((8, C), F32), jnp.concatenate([present, jnp.zeros((C - GQ, C), F32)], axis=0), NT, EXACT)
    f_src[0] = sums
    f_src[1] = pltpu.roll(sums, C - 16, 1)
    send_to(a_peers, lambda peer: f_src.at[peer[0] // 2 % 2], value_hbm.at[sc], f_sems)
    small_ref[0:16, :] = 100.0 * jnp.where(zh == 0, credited[:16], credited[16:])
    late = [
        pltpu.make_async_copy(src, dst, load_sem.at[4 + n])
        for n, (src, dst) in enumerate(
            [
                (small_ref, small_hbm),
                (f_src.at[zh], value_hbm.at[sc]),
                (d_src.at[0], rho_hbm.at[0, mine, :]),
                (d_src.at[1], rho_hbm.at[1, mine, :]),
            ]
        )
    ]
    for store in late:
        store.start()
    for exchange in (a_all, e_all, b_all, c_all):
        exchange.wait_send()
    for store in stores + late:
        store.wait()
    for exchange in (*d_alls, f_all):
        exchange.wait_send()
        exchange.wait_recv()


CHUNK = 16


def output_kernel(
    rho_hbm, pre_hbm, table_hbm, lapse1_hbm, small_hbm, value_hbm,
    occupancy_hbm, account_hbm, credited_hbm, out_value_hbm,
    rho_ref, pre_ref, table_ref, lapse1_ref, point_ref, small_ref, sums_ref,
    occupancy_ref, account_ref, value_ref, load_sem, store_sem,
):
    loads = [
        pltpu.make_async_copy(src, dst, load_sem.at[n])
        for n, (src, dst) in enumerate(
            [
                (table_hbm, table_ref),
                (rho_hbm, rho_ref),
                (pre_hbm, pre_ref),
                (small_hbm, small_ref),
                (lapse1_hbm.at[:CHUNK], lapse1_ref.at[:CHUNK]),
                (lapse1_hbm.at[CHUNK:], lapse1_ref.at[CHUNK:]),
                (value_hbm, sums_ref),
            ]
        )
    ]
    for load in loads:
        load.start()
    loads[0].wait()
    labels = group_at(iota((PG, TILE), 0)).astype(F32)
    for tile in range(M // TILE):
        at = pl.ds(tile * TILE, TILE)
        point_ref[:, at] = (labels == table_ref[36:37, at]).astype(BF16)
    for load in loads[1:4]:
        load.wait()
    copies = [pltpu.make_async_copy(small_ref.at[0:16, :], credited_hbm, store_sem.at[2])]
    copies[0].start()
    twice = pre_ref[0]
    rho = [pre_ref[1], rho_ref[0], rho_ref[1]]
    tables = []
    for month in (1, 2):
        rates = small_ref[24 + month : 25 + month, :]
        tables.append(twice * jax.nn.sigmoid(LAPSE_SLOPE * (rates - rho[month])))
    grown = [rate * (1.0 / 12.0) for rate in rho]
    gain = grown[0] + grown[1] + grown[0] * grown[1]
    tables.append(gain + grown[2] + gain * grown[2])
    tables = [parts(jnp.transpose(table), 2) for table in tables]

    loads[4].wait()
    for chunk in range(C // CHUNK):
        rows = slice(chunk * CHUNK, (chunk + 1) * CHUNK)
        lhs = jnp.concatenate([piece[rows] for table in tables for piece in table], axis=0)
        for tile in range(M // TILE):
            at = pl.ds(tile * TILE, TILE)
            found = dot(lhs, point_ref[:, at], NN)
            found = [
                found[2 * n * CHUNK : (2 * n + 1) * CHUNK] + found[(2 * n + 1) * CHUNK : (2 * n + 2) * CHUNK]
                for n in range(3)
            ]
            first = lapse1_ref[rows, at]
            second = (table_ref[33:34, at] - first * table_ref[24:25, at]) * found[0]
            third = (table_ref[34:35, at] - first * table_ref[16:17, at] - second * table_ref[24:25, at]) * found[1]
            for u in range(S):
                occupancy_ref[u, rows, at] = (
                    table_ref[u : u + 1, at]
                    - first * table_ref[8 + u : 9 + u, at]
                    - second * table_ref[16 + u : 17 + u, at]
                    - third * table_ref[24 + u : 25 + u, at]
                )
            account = table_ref[35:36, at]
            account_ref[rows, at] = account + account * found[2]
        pltpu.make_async_copy(occupancy_ref.at[:, rows, :], occupancy_hbm.at[:, rows, :], store_sem.at[0]).start()
        pltpu.make_async_copy(account_ref.at[rows, :], account_hbm.at[rows, :], store_sem.at[1]).start()
        if chunk == 0:
            for load in loads[5:]:
                load.wait()
            value = sums_ref[0]
            for slot in range(1, SC):
                value = value + sums_ref[slot]
            value_ref[...] = value[0:1, 0:16] * (1.0 / SCEN)
            copies.append(pltpu.make_async_copy(value_ref, out_value_hbm, store_sem.at[3]))
            copies[-1].start()
    copies.append(pltpu.make_async_copy(occupancy_ref, occupancy_hbm, store_sem.at[0]))
    copies.append(pltpu.make_async_copy(account_ref, account_hbm, store_sem.at[1]))
    for copy in copies:
        copy.wait()


def vmem(*shape):
    return pltpu.VMEM(shape, F32)


def body(
    group_id,
    issue_state,
    account_start,
    transition,
    lapse_base,
    benefit,
    bond_block,
    bond_flows,
    bond_target,
    base_rate,
    rate_moves,
    guarantee,
    spread,
    start_rate,
):
    in_hbm = pl.BlockSpec(memory_space=pltpu.HBM)
    dma = pltpu.SemaphoreType.DMA
    between = pl.pallas_call(
        exchange_kernel,
        out_shape=[
            jax.ShapeDtypeStruct((2, PG, C), F32),
            jax.ShapeDtypeStruct((2, PG, C), F32),
            jax.ShapeDtypeStruct((40, M), F32),
            jax.ShapeDtypeStruct((C, M), F32),
            jax.ShapeDtypeStruct((32, C), F32),
            jax.ShapeDtypeStruct((SC, 8, C), F32),
        ],
        in_specs=[in_hbm] * 14,
        out_specs=[in_hbm] * 6,
        scratch_shapes=[
            vmem(2, PG, C),
            vmem(40, M),
            vmem(C, M),
            vmem(32, C),
            vmem(1, C),
            vmem(MONTHS, C),
            pltpu.VMEM((1, B), jnp.int32),
            vmem(B, K),
            pltpu.VMEM((1, M), jnp.int32),
            pltpu.VMEM((1, M), jnp.int32),
            vmem(1, M),
            vmem(S, S, PG),
            vmem(1, S),
            vmem(1, PG),
            vmem(1, PG),
            vmem(1, PG),
            vmem(B // C, C),
            vmem(C, PG),
            pltpu.VMEM((2, K, B), BF16),
            vmem(KD, B),
            pltpu.VMEM((PG, B), BF16),
            pltpu.VMEM((PG, M), BF16),
            pltpu.VMEM((DATES, 3, K, C), BF16),
            vmem(PG, 8),
            vmem(PG, C),
            vmem(8, C),
            vmem(SC, 8, C),
            vmem(MP // 2, 8, C),
            vmem(MP, 8, C),
            vmem(MP // 2, KD, C),
            vmem(MP, KD, C),
            vmem(K, C),
            vmem(2, GQ, C),
            vmem(2, 8, C),
            dma((14,)),
            *[dma((2,)) for _ in range(7)],
        ],
        compiler_params=pltpu.CompilerParams(
            collective_id=0, has_side_effects=True, vmem_limit_bytes=VMEM_LIMIT
        ),
        name="exchange",
    )(
        base_rate.reshape(1, C),
        rate_moves,
        bond_block.reshape(1, B),
        bond_flows,
        group_id.reshape(1, M),
        issue_state.reshape(1, M),
        account_start.reshape(1, M),
        transition.transpose(1, 2, 0),
        benefit.reshape(1, S),
        guarantee.reshape(1, PG),
        spread.reshape(1, PG),
        lapse_base.reshape(1, PG),
        bond_target.reshape(B // C, C),
        start_rate,
    )
    occupancy, account_value, credited, value = pl.pallas_call(
        output_kernel,
        out_shape=[
            jax.ShapeDtypeStruct((S, C, M), F32),
            jax.ShapeDtypeStruct((C, M), F32),
            jax.ShapeDtypeStruct((16, C), F32),
            jax.ShapeDtypeStruct((1, 16), F32),
        ],
        in_specs=[in_hbm] * 6,
        out_specs=[in_hbm] * 4,
        scratch_shapes=[
            vmem(2, PG, C),
            vmem(2, PG, C),
            vmem(40, M),
            vmem(C, M),
            pltpu.VMEM((PG, M), BF16),
            vmem(32, C),
            vmem(SC, 8, C),
            vmem(S, C, M),
            vmem(C, M),
            vmem(1, 16),
            dma((7,)),
            dma((4,)),
        ],
        compiler_params=pltpu.CompilerParams(vmem_limit_bytes=VMEM_LIMIT),
        name="outputs",
    )(*between)
    return occupancy, account_value, credited.T, value.reshape(16)


def solution(mesh):
    placed = (
        P("mp"),
        P("mp"),
        P("mp"),
        P(),
        P(),
        P(),
        P("mp", None),
        P("mp", None),
        P("mp"),
        P("scen"),
        P(None, "scen"),
        P(),
        P(),
        P("scen", None),
    )
    return jax.shard_map(
        body,
        mesh=mesh,
        in_specs=placed,
        out_specs=(P(None, "scen", "mp"), P("scen", "mp"), P("scen", "mp"), P("mp")),
        check_vma=False,
    )
```
